512 devices in a mesh: pipe: 8 (over y_lo, x), expert: 16 (over z, core), dp: 4 (over y_hi).
Axes of the slice: x: 4, y: 8 (y_hi: 4, y_lo: 2; y = y_hi * 2 + y_lo), z: 8, core: 2. Of those that a mesh axis runs over, the one named last changes fastest.
Arguments:
- in_flight: bfloat16 [8, 4096, 2048], P('pipe', ('expert', 'dp')), may hold values from -6 to 6
- fresh_grads: bfloat16 [1, 4096, 2048], P(None, ('expert', 'dp')), may hold values from -6 to 6
- saved_inputs: bfloat16 [2, 8, 4096, 2048], P(None, 'pipe', ('expert', 'dp')), may hold values from -6 to 6
- norm_gain: bfloat16 [8, 2048], P('pipe'), may hold values from 0.099609375 to 1.8984375
- expert_ids: int32 [2, 8, 4096, 2], P(None, 'pipe', ('expert', 'dp')), may hold values from 0 to 7, all different within a row; in each aligned block of 64 rows (0 to 63, 64 to 127, ..., all dimensions but the last counted through in order) at most 24 rows name the same one
- gate_weights: float32 [2, 8, 4096, 2], P(None, 'pipe', ('expert', 'dp')), may hold values from 0.1 to 1
- up_weights: bfloat16 [8, 5632, 2048], P('pipe', 'expert'), may hold values from -0.125 to 0.125
- down_weights: bfloat16 [8, 5632, 2048], P('pipe', 'expert'), may hold values from -0.21875 to 0.21875
Outputs:
- input_grads: bfloat16 [2, 8, 4096, 2048], P(None, 'pipe', ('expert', 'dp'))
- up_grads: bfloat16 [8, 5632, 2048], P('pipe', 'expert', 'dp')
- down_grads: bfloat16 [8, 5632, 2048], P('pipe', 'expert', 'dp')
The draws below stay inside these ranges and needn't reach their ends.
Inputs may be any that keep to these rules, and one draw needn't show every extreme that they name: `expert_ids`: each row names two different experts. Among the 64 frames of one device's aligned block of one step and section, no expert is named more than 24 times, a bound that some block reaches.
All inputs are finite; a program needn't handle non-finite values.
Results may differ from the reference program's by a relative error of at most 0.015.
Values may be sent and summed in bfloat16 or wider, within the bound.
A program may use at most 64 MiB of HBM per device.

```python
import math
import jax
import jax.numpy as jnp
import numpy as np
from jax import lax

D = 2048
H = 704
TOK_DEV = 64
STEPS = 2
SECTIONS = 8
EXPERTS = 8
CAP = 24
TOKENS = 4096
N_EXPERT = 16
N_DP = 4


def level_of(stream_key, dims, split, smallest, high):
    def one(axis_at, shards_of):
        draws = jax.random.uniform(jax.random.fold_in(jax.random.fold_in(stream_key, 6), axis_at), (shards_of,), jnp.float32, smallest / len(split), high / len(split))
        return jnp.repeat(jnp.exp(draws), dims[axis_at] // shards_of).reshape((-1,) + (1,) * (len(dims) - axis_at - 1))

    level = one(*split[0])
    for cut in split[1:]:
        level = level * one(*cut)
    return level


def routed_block(rng, own, number, rows, amount, top, reach, skew):
    ranking = jax.random.permutation(rng, amount)
    packed, ordinary = portions_of(amount, rows * top, reach, skew, True), portions_of(amount, rows * top, reach, skew, False)
    places = jnp.arange(amount)

    def named(tallies, rotation):
        used = int((tallies > 0).sum())
        fixed = max(1, used // 4)
        shifted = fixed + (places - fixed + rotation * (used - fixed)) % max(1, amount - fixed)
        return jnp.zeros((amount,), jnp.int32).at[ranking[jnp.where(places < fixed, places, shifted)]].set(jnp.asarray(tallies, jnp.int32))

    tallies = jnp.where(number % 4 == 0, named(packed, number // 4), named(ordinary, number - number // 4 - 1))
    mixed = jax.random.permutation(jax.random.fold_in(own, 3), amount)
    source_of, receiver = mixed[0:amount // 2 * 2:2], mixed[1:amount // 2 * 2:2]
    slack = jnp.minimum(tallies[source_of] - 1, reach - tallies[receiver]) // 2
    slack = jnp.where((source_of == ranking[0]) | (receiver == ranking[0]) | (tallies[receiver] == 0), 0, jnp.maximum(slack, 0))
    shifted = jax.random.randint(jax.random.fold_in(own, 4), (amount // 2,), 0, 1 << 20) % (slack + 1)
    tallies = tallies.at[source_of].add(-shifted).at[receiver].add(shifted)
    members = jnp.searchsorted(jnp.cumsum(tallies), jnp.arange(rows * top), side="right").astype(jnp.int32)
    grid = members.reshape(top, rows).T
    grid = grid[jax.random.permutation(jax.random.fold_in(own, 1), rows)]
    rotation = jax.random.randint(jax.random.fold_in(own, 2), (rows, 1), 0, top)
    return jnp.take_along_axis(grid, (jnp.arange(top)[None, :] + rotation) % top, axis=1)


def portions_of(count, total, reach, lean, full):
    loads = [(1 << 20) // math.isqrt(grade ** lean) + 1 for grade in range(1, count + 1)]
    largest = reach if full else min(reach, max(-(-total // count), total * loads[0] // sum(loads)))
    least = 1 if total - largest >= count - 1 else 0
    holding, surplus = [largest] + [least] * (count - 1), total - largest - least * (count - 1)
    while surplus > 0:
        movable = [i for i in range(1, count) if holding[i] < largest] or [i for i in range(1, count) if holding[i] < reach]
        mass, remaining = sum([loads[i] for i in movable]), surplus
        for i in movable:
            addition = min(reach - holding[i], max(1, remaining * loads[i] // mass), surplus)
            holding[i] = holding[i] + addition
            surplus = surplus - addition
    return np.array(holding)


def gaussian(own_key, dims, scale, most, shards=(), kind=jnp.bfloat16):
    drawn = jax.random.normal(own_key, dims, jnp.float32) * scale
    if len(shards) > 0:
        drawn = level_of(own_key, dims, shards, -0.22, 0.18) * drawn
    return jnp.clip(drawn, min=-most, max=most).astype(kind)


def setup_inputs(seed: int = 0) -> dict:
    keys = jax.random.split(jax.random.key(seed), 9)
    in_flight = gaussian(keys[0], (SECTIONS, TOKENS, D), 1.0, 6.0, ((0, 8), (1, 64)))
    fresh_grads = gaussian(keys[1], (STEPS - 1, TOKENS, D), 1.0, 6.0, ((1, 64),))
    saved_inputs = gaussian(keys[2], (STEPS, SECTIONS, TOKENS, D), 1.0, 6.0, ((1, 8), (2, 64)))
    norm_gain = jnp.clip(1.0 + 0.18 * jax.random.normal(keys[3], (SECTIONS, D), jnp.float32), 0.099609375, 1.8984375).astype(jnp.bfloat16)
    expert_ids_keys = jax.random.split(jax.random.fold_in(keys[4], 1), STEPS * SECTIONS * TOKENS // TOK_DEV)
    expert_ids_turns = jax.random.permutation(jax.random.fold_in(keys[4], 3), STEPS * SECTIONS * TOKENS // TOK_DEV)
    expert_ids = jax.vmap(lambda own, number: routed_block(jax.random.fold_in(keys[4], 2), own, number, TOK_DEV, EXPERTS, 2, CAP, 2))(expert_ids_keys, expert_ids_turns).reshape((STEPS, SECTIONS, TOKENS, 2))
    gate_weights = jnp.clip(0.1 + 0.9 * jax.random.uniform(keys[5], (STEPS, SECTIONS, TOKENS, 2), jnp.float32) ** level_of(keys[5], (STEPS, SECTIONS, TOKENS, 2), ((1, 8), (2, 64)), -0.2, 0.2), 0.1, 1.0)
    up_weights = gaussian(keys[6], (SECTIONS, EXPERTS * H, D), D ** -0.5, 0.125, ((0, 8), (1, 16)))
    down_weights = gaussian(keys[7], (SECTIONS, EXPERTS * H, D), H ** -0.5, 0.21875, ((0, 8), (1, 16)))
    return {"in_flight": in_flight, "fresh_grads": fresh_grads, "saved_inputs": saved_inputs, "norm_gain": norm_gain, "expert_ids": expert_ids, "gate_weights": gate_weights, "up_weights": up_weights, "down_weights": down_weights}


norm_eps = 1e-06

def layer_back(incoming, saved, gain, chosen_ids, gates, up_section, down_section):
    inputs = saved.astype(jnp.float32)
    scale = lax.rsqrt(lax.optimization_barrier(jnp.mean(inputs * inputs, axis=-1, keepdims=True)) + norm_eps)
    normed = (inputs * scale * gain.astype(jnp.float32)).astype(jnp.bfloat16)
    scaled = (gates[:, :, None] * incoming.astype(jnp.float32)[:, None, :]).astype(jnp.bfloat16)
    scaled = scaled.reshape(2 * TOKENS, D)
    normed_pairs = jnp.repeat(normed, 2, axis=0)
    zero_row = jnp.zeros((1, D), jnp.bfloat16)
    normed_pad = jnp.concatenate([normed_pairs, zero_row], 0)
    scaled_pad = jnp.concatenate([scaled, zero_row], 0)
    flat_ids = chosen_ids.reshape(-1)
    replica = jnp.arange(2 * TOKENS, dtype=jnp.int32) // 2 // TOK_DEV % N_DP
    half_units = H // 2

    def one_item(item_index):
        expert_index = item_index // N_DP
        replica_index = item_index % N_DP
        chosen = (flat_ids == expert_index) & (replica == replica_index)
        positions = jnp.nonzero(chosen, size=N_EXPERT * CAP, fill_value=2 * TOKENS)[0].astype(jnp.int32)
        slot_inputs = normed_pad[positions]
        slot_grads = scaled_pad[positions]
        up_rows = lax.dynamic_slice_in_dim(up_section, (expert_index * H).astype(jnp.int32), H, 0)
        down_rows = lax.dynamic_slice_in_dim(down_section, (expert_index * H).astype(jnp.int32), H, 0)
        pre_act = lax.dot_general(slot_inputs, up_rows, (((1,), (1,)), ((), ())), preferred_element_type=jnp.float32)
        sigma = jax.nn.sigmoid(pre_act)
        activated = (pre_act * sigma).astype(jnp.bfloat16)
        hidden_grad = lax.dot_general(slot_grads, down_rows, (((1,), (1,)), ((), ())), preferred_element_type=jnp.float32)
        hidden_grad = (hidden_grad * (sigma * (1.0 + pre_act * (1.0 - sigma)))).astype(jnp.bfloat16)
        first_part = jnp.dot(hidden_grad[:, :half_units], up_rows[:half_units], preferred_element_type=jnp.float32)
        second_part = jnp.dot(hidden_grad[:, half_units:], up_rows[half_units:], preferred_element_type=jnp.float32)
        first_part = lax.optimization_barrier(first_part.astype(jnp.bfloat16)).astype(jnp.float32)
        second_part = lax.optimization_barrier(second_part.astype(jnp.bfloat16)).astype(jnp.float32)
        up_part = lax.dot_general(hidden_grad, slot_inputs, (((0,), (0,)), ((), ())), preferred_element_type=jnp.float32)
        down_part = lax.dot_general(activated, slot_grads, (((0,), (0,)), ((), ())), preferred_element_type=jnp.float32)
        return (positions, first_part + second_part, up_part, down_part)
    positions, feature_parts, up_part, down_part = lax.map(one_item, jnp.arange(EXPERTS * N_DP, dtype=jnp.int32))
    gathered = jnp.zeros((2 * TOKENS + 1, D), jnp.float32).at[positions.reshape(-1)].add(feature_parts.reshape(-1, D))
    feature_grad = gathered[:2 * TOKENS].reshape(TOKENS, 2, D).sum(axis=1)
    weighted = gain.astype(jnp.float32) * feature_grad
    result = incoming.astype(jnp.float32) + scale * weighted
    result = result - inputs * (scale * scale * scale) * lax.optimization_barrier(jnp.mean(inputs * weighted, axis=-1, keepdims=True))
    return (result.astype(jnp.bfloat16), up_part.reshape(EXPERTS, N_DP, H, D), down_part.reshape(EXPERTS, N_DP, H, D))

def finish(totals):
    rounded = lax.optimization_barrier(totals.astype(jnp.bfloat16)).astype(jnp.float32)
    return lax.optimization_barrier(jnp.sum(rounded, axis=1)).astype(jnp.bfloat16).reshape(EXPERTS * H, D)

def reference(in_flight, fresh_grads, saved_inputs, norm_gain, expert_ids, gate_weights, up_weights, down_weights):
    grads_by_step = [[None] * SECTIONS for step_index in range(STEPS)]
    up_list = []
    down_list = []
    for section_index in range(SECTIONS - 1, -1, -1):
        up_total = jnp.zeros((EXPERTS, N_DP, H, D), jnp.float32)
        down_total = jnp.zeros((EXPERTS, N_DP, H, D), jnp.float32)
        for step_index in range(STEPS):
            if step_index == 0:
                incoming = in_flight[section_index]
            elif section_index == SECTIONS - 1:
                incoming = fresh_grads[step_index - 1]
            else:
                incoming = grads_by_step[step_index - 1][section_index + 1]
            result, up_part, down_part = layer_back(incoming, saved_inputs[step_index, section_index], norm_gain[section_index], expert_ids[step_index, section_index], gate_weights[step_index, section_index], up_weights[section_index], down_weights[section_index])
            grads_by_step[step_index][section_index] = result
            up_total = up_total + up_part
            down_total = down_total + down_part
        up_list.insert(0, finish(up_total))
        down_list.insert(0, finish(down_total))
    input_grads = jnp.stack([jnp.stack(grads_by_step[step_index], 0) for step_index in range(STEPS)], 0)
    return (input_grads, jnp.stack(up_list, 0), jnp.stack(down_list, 0))
```

```python
import functools

import jax
import jax.numpy as jnp
from jax import lax
from jax.experimental import pallas as pl
from jax.experimental.pallas import tpu as pltpu
from jax.sharding import PartitionSpec as P

norm_eps = 1e-06
MESH = pl.DeviceIdType.MESH
f32 = jnp.float32
bf16 = jnp.bfloat16


def dot(left, right, left_dim, right_dim):
    return lax.dot_general(
        left, right, (((left_dim,), (right_dim,)), ((), ())), preferred_element_type=f32
    )


def kernel(
    chips,
    replicas,
    sections,
    capacity,
    in_flight,
    fresh,
    saved,
    gain,
    ids,
    gates,
    up_hbm,
    down_hbm,
    out_grads,
    out_up,
    out_down,
    up_w,
    down_w,
    select,
    gate_of,
    frames,
    scales,
    snd,
    own,
    sib,
    x_all,
    g_all,
    act_all,
    hid_all,
    slope,
    part_own,
    part_snd,
    part_rcv,
    ret_snd,
    ret_rcv,
    relay_snd,
    relay_rcv,
    rs_snd,
    rs_rcv,
    w_sem,
    disp_s,
    disp_r,
    fwd_s,
    fwd_r,
    part_s,
    part_r,
    ret_s,
    ret_r,
    relay_s,
    relay_r,
    rs_s,
    rs_r,
):
    n, cap = chips, capacity
    block = 2 * cap
    rows, half = frames.shape[2], frames.shape[3]
    tokens = rows // 2
    per_step = n * block
    group = n // 4
    group_rows = 2 * group * cap
    quarter = out_up.shape[2]
    place = lax.axis_index("expert")
    chip, core = place // 2, lax.rem(place, 2)
    section = lax.axis_index("pipe")
    replica = lax.axis_index("dp")

    def chip_at(d):
        return {"expert": 2 * lax.rem(chip + d, n) + core}

    sibling = {"expert": 2 * chip + 1 - core}
    section_before = {"pipe": lax.rem(section + sections - 1, sections)}
    section_after = {"pipe": lax.rem(section + 1, sections)}
    replica_after = {"dp": lax.rem(replica + 1, replicas)}
    replica_before = {"dp": lax.rem(replica + replicas - 1, replicas)}

    def remote(src, dst, s_sem, r_sem, to):
        return pltpu.make_async_remote_copy(
            src_ref=src,
            dst_ref=dst,
            send_sem=s_sem,
            recv_sem=r_sem,
            device_id=to,
            device_id_type=MESH,
        )

    load_up = pltpu.make_async_copy(up_hbm.at[0], up_w, w_sem.at[0])
    load_down = pltpu.make_async_copy(down_hbm.at[0], down_w, w_sem.at[1])
    load_up.start()
    load_down.start()

    barrier = pltpu.get_barrier_semaphore()
    partners = [chip_at(d) for d in range(1, n)]
    partners += [sibling, section_before, section_after, replica_after, replica_before]
    for partner in partners:
        pl.semaphore_signal(barrier, inc=1, device_id=partner, device_id_type=MESH)

    def stacked(ref, *at):
        left = ref[(*at, slice(None), slice(0, half))]
        right = ref[(*at, slice(None), slice(half, 2 * half))]
        return jnp.concatenate([left.astype(f32), right.astype(f32)], axis=0)

    gain_row = gain[...].astype(f32)
    gain_two = jnp.concatenate(
        [
            jnp.broadcast_to(gain_row[:, :half], (tokens, half)),
            jnp.broadcast_to(gain_row[:, half:], (tokens, half)),
        ],
        axis=0,
    )

    def feature_mean(values):
        sums = jnp.sum(values, axis=1, keepdims=True)
        both = (sums[:tokens] + sums[tokens:]) * (1.0 / (2 * half))
        return jnp.concatenate([both, both], axis=0)

    def routing(step):
        eye = lax.broadcasted_iota(jnp.int32, (rows, rows), 0) == lax.broadcasted_iota(
            jnp.int32, (rows, rows), 1
        )

        def as_row(column):
            both = jnp.concatenate([column, column], axis=0)
            return jnp.sum(jnp.where(eye, both, 0.0), axis=0, keepdims=True)

        id_rows = [as_row(ids[step, 0, :, j : j + 1].astype(f32)) for j in range(2)]
        gate_rows = [as_row(gates[step, 0, :, j : j + 1]) for j in range(2)]
        expert = lax.rem(lax.broadcasted_iota(jnp.int32, (n, rows), 0) + chip, n).astype(f32)
        named = [id_rows[j] == expert for j in range(2)]
        member = jnp.where(named[0] | named[1], 1.0, 0.0)
        gate = jnp.where(named[0], gate_rows[0], 0.0) + jnp.where(named[1], gate_rows[1], 0.0)
        r0 = lax.broadcasted_iota(jnp.int32, (rows, rows), 0)
        r1 = lax.broadcasted_iota(jnp.int32, (rows, rows), 1)
        before = (r0 < tokens) & (r0 < lax.rem(r1, tokens))
        slot = dot(member.astype(bf16), jnp.where(before, 1.0, 0.0).astype(bf16), 1, 0)
        at = lax.broadcasted_iota(jnp.int32, (block, rows), 0)
        lane = lax.broadcasted_iota(jnp.int32, (block, rows), 1)
        same_half = (at >= cap) == (lane >= tokens)
        at_slot = jnp.where(at >= cap, at - cap, at).astype(f32)
        for d in range(n):
            hit = same_half & (member[d : d + 1] > 0.5) & (slot[d : d + 1] == at_slot)
            select[step, d * block : (d + 1) * block, :] = jnp.where(hit, 1.0, 0.0).astype(bf16)
            gate_of[step, d * block : (d + 1) * block, :] = jnp.sum(
                jnp.where(hit, gate[d : d + 1], 0.0), axis=1, keepdims=True
            )

    def normed_frames(step):
        inputs = stacked(saved, step, 0)
        scale = lax.rsqrt(feature_mean(inputs * inputs) + norm_eps)
        scales[step] = scale
        return (inputs * scale * gain_two).astype(bf16)

    def fill(which, step, values, gated):
        for d in range(n):
            at = slice(d * block, (d + 1) * block)
            picked = dot(select[step, at, :], values, 1, 0)
            if gated:
                picked = picked * gate_of[step, at, :]
            target = own.at[which, 0] if d == 0 else snd.at[which, d]
            target[...] = picked.astype(bf16)

    def dispatch(which, d):
        return remote(
            snd.at[which, d],
            own.at[which, d],
            disp_s.at[which, d],
            disp_r.at[which, d],
            chip_at(d),
        )

    def forward(which, d):
        return remote(
            own.at[which, d], sib.at[which, d], fwd_s.at[which, d], fwd_r.at[which, d], sibling
        )

    order = []
    for k in range(1, n // 2):
        order += [n // 2 - k, n // 2 + k]
    order = [n // 2] + order

    def send_all(which):
        for d in order:
            dispatch(which, d).start()

    near_first = [0]
    for k in range(1, n // 2):
        near_first += [k, n - k]
    near_first += [n // 2]
    groups = [near_first[g * group : (g + 1) * group] for g in range(4)]

    def receive(which, g):
        for d in groups[g]:
            if d != 0:
                dispatch(which, d).wait_recv()
            forward(which, d).start()

    def unpack(which, g, target, first_row):
        for side, source in enumerate((own, sib)):
            if side == 1:
                for d in groups[g]:
                    forward(which, d).wait_recv()
            pieces = [source[which, d].astype(f32) for d in groups[g]]
            at = first_row + side * group * cap
            left = jnp.concatenate([p[:cap] for p in pieces], axis=0)
            right = jnp.concatenate([p[cap:] for p in pieces], axis=0)
            target[at : at + group * cap, 0:half] = left.astype(bf16)
            target[at : at + group * cap, half : 2 * half] = right.astype(bf16)

    def normed_phase(step):
        which = 2 * step
        receive(which, 0)
        for g in range(4):
            if g < 3:
                receive(which, g + 1)
            first = step * per_step + g * group_rows
            unpack(which, g, x_all, first)
            at = slice(first, first + group_rows)
            pre = dot(x_all[at, :], up_w[...], 1, 1)
            sigma = jax.nn.sigmoid(pre)
            act_all[at, :] = (pre * sigma).astype(bf16)
            slope[g * group_rows : (g + 1) * group_rows, :] = sigma * (1.0 + pre * (1.0 - sigma))

    def part_copy(step, g):
        return remote(
            part_snd.at[step, g],
            part_rcv.at[step, g],
            part_s.at[step, g],
            part_r.at[step, g],
            sibling,
        )

    def returning(step, d):
        return remote(
            ret_snd.at[step, d],
            ret_rcv.at[step, d],
            ret_s.at[step, d],
            ret_r.at[step, d],
            chip_at(n - d),
        )

    def finish_part(step, g):
        part_copy(step, g).wait_recv()
        total = part_own[g] + part_rcv[step, g].astype(f32)
        for k, d in enumerate(groups[g]):
            piece = total[k * cap : (k + 1) * cap]
            packed = jnp.concatenate([piece[:, :half], piece[:, half:]], axis=0).astype(bf16)
            if d == 0:
                ret_rcv[step, 0] = packed
            else:
                ret_snd[step, d] = packed
                returning(step, d).start()

    def grads_phase(step):
        which = 2 * step + 1
        receive(which, 0)
        for g in range(4):
            if g < 3:
                receive(which, g + 1)
            first = step * per_step + g * group_rows
            unpack(which, g, g_all, first)
            at = slice(first, first + group_rows)
            back = dot(g_all[at, :], down_w[...], 1, 1)
            hidden = (back * slope[g * group_rows : (g + 1) * group_rows, :]).astype(bf16)
            hid_all[at, :] = hidden
            part = dot(hidden, up_w[...], 1, 0)
            part_own[g] = part[: group * cap]
            part_snd[step, g] = part[group * cap :].astype(bf16)
            part_copy(step, g).start()
            if g > 0:
                finish_part(step, g - 1)

    def finish_step(step, incoming):
        for d in range(1, n):
            returning(step, d).wait_recv()
        back = ret_rcv[step].reshape(n * block, half)
        weighted = gain_two * dot(select[step], back, 0, 0)
        inputs = stacked(saved, step, 0)
        scale = scales[step]
        result = incoming + scale * weighted
        result = result - inputs * (scale * scale * scale) * feature_mean(inputs * weighted)
        result = result.astype(bf16)
        out_grads[step, 0, :, 0:half] = result[:tokens]
        out_grads[step, 0, :, half : 2 * half] = result[tokens:]
        return result

    routing(0)
    fill(0, 0, normed_frames(0), False)
    pl.semaphore_wait(barrier, len(partners))
    send_all(0)
    frames[0, 0] = stacked(in_flight, 0).astype(bf16)
    fill(1, 0, frames[0, 0], True)
    send_all(1)
    routing(1)
    fill(2, 1, normed_frames(1), False)

    load_up.wait()
    normed_phase(0)
    load_down.wait()
    grads_phase(0)
    finish_part(0, 3)

    result = finish_step(0, frames[0, 0].astype(f32))
    send_all(2)
    relay_snd[...] = result
    relay = remote(relay_snd, relay_rcv, relay_s, relay_r, section_before)
    relay.start()
    relay.wait_recv()
    last = section == sections - 1
    frames[0, 1] = jnp.where(
        last, stacked(fresh, 0), relay_rcv[...].astype(f32)
    ).astype(bf16)
    fill(3, 1, frames[0, 1], True)
    send_all(3)
    normed_phase(1)
    grads_phase(1)

    def slice_of(left, right, k):
        owner = lax.rem(replica + k, replicas)
        columns = pl.ds(pl.multiple_of(owner * quarter, quarter), quarter)
        return dot(left[...], right[:, columns], 0, 0)

    def reduce_copy(i, to):
        return remote(rs_snd.at[i], rs_rcv.at[i], rs_s.at[i], rs_r.at[i], to)

    copies = [
        reduce_copy(0, replica_before),
        reduce_copy(1, replica_after),
        reduce_copy(2, replica_after),
        reduce_copy(3, replica_before),
        reduce_copy(4, replica_after),
        reduce_copy(5, replica_before),
    ]

    def down_slice(k):
        return slice_of(act_all, g_all, k)

    def up_slice(k):
        return slice_of(hid_all, x_all, k)

    def put(i, value):
        rs_snd[i] = value.astype(bf16)
        copies[i].start()

    put(0, down_slice(2))
    put(1, down_slice(1))
    finish_part(1, 3)
    put(2, up_slice(2))
    put(3, up_slice(3))
    down_near = down_slice(3)
    copies[0].wait_recv()
    put(5, down_near + rs_rcv[0].astype(f32))
    up_near = up_slice(1)
    copies[2].wait_recv()
    put(4, up_near + rs_rcv[2].astype(f32))

    finish_step(1, frames[0, 1].astype(f32))

    down_mine = down_slice(0)
    copies[1].wait_recv()
    copies[5].wait_recv()
    out_down[0] = (down_mine + rs_rcv[1].astype(f32) + rs_rcv[5].astype(f32)).astype(bf16)
    up_mine = up_slice(0)
    copies[3].wait_recv()
    copies[4].wait_recv()
    out_up[0] = (up_mine + rs_rcv[3].astype(f32) + rs_rcv[4].astype(f32)).astype(bf16)

    for which in range(4):
        for d in range(n):
            if d != 0:
                dispatch(which, d).wait_send()
            forward(which, d).wait_send()
    for step in range(2):
        for g in range(4):
            part_copy(step, g).wait_send()
        for d in range(1, n):
            returning(step, d).wait_send()
    relay.wait_send()
    for copy in copies:
        copy.wait_send()


def local(
    mesh_sizes,
    in_flight,
    fresh_grads,
    saved_inputs,
    norm_gain,
    expert_ids,
    gate_weights,
    up_weights,
    down_weights,
):
    sections, places, replicas = mesh_sizes
    chips = places // 2
    tokens, width = saved_inputs.shape[2:]
    hidden = up_weights.shape[1]
    cap = min(tokens, 3 * tokens // chips)
    half = width // 2
    block = 2 * cap
    per_step = chips * block
    group_slots = per_step // 8
    quarter = width // replicas
    vmem = pl.BlockSpec(memory_space=pltpu.VMEM)
    anywhere = pl.BlockSpec(memory_space=pl.ANY)
    dma = pltpu.SemaphoreType.DMA
    scratch = [
        pltpu.VMEM((hidden, width), bf16),
        pltpu.VMEM((hidden, width), bf16),
        pltpu.VMEM((2, chips * block, 2 * tokens), bf16),
        pltpu.VMEM((2, chips * block, 1), f32),
        pltpu.VMEM((1, 2, 2 * tokens, half), bf16),
        pltpu.VMEM((2, 2 * tokens, 1), f32),
        pltpu.VMEM((4, chips, block, half), bf16),
        pltpu.VMEM((4, chips, block, half), bf16),
        pltpu.VMEM((4, chips, block, half), bf16),
        pltpu.VMEM((2 * per_step, width), bf16),
        pltpu.VMEM((2 * per_step, width), bf16),
        pltpu.VMEM((2 * per_step, hidden), bf16),
        pltpu.VMEM((2 * per_step, hidden), bf16),
        pltpu.VMEM((per_step, hidden), f32),
        pltpu.VMEM((4, group_slots, width), f32),
        pltpu.VMEM((2, 4, group_slots, width), bf16),
        pltpu.VMEM((2, 4, group_slots, width), bf16),
        pltpu.VMEM((2, chips, block, half), bf16),
        pltpu.VMEM((2, chips, block, half), bf16),
        pltpu.VMEM((2 * tokens, half), bf16),
        pltpu.VMEM((2 * tokens, half), bf16),
        pltpu.VMEM((6, hidden, quarter), bf16),
        pltpu.VMEM((6, hidden, quarter), bf16),
        dma((2,)),
        dma((4, chips)),
        dma((4, chips)),
        dma((4, chips)),
        dma((4, chips)),
        dma((2, 4)),
        dma((2, 4)),
        dma((2, chips)),
        dma((2, chips)),
        dma,
        dma,
        dma((6,)),
        dma((6,)),
    ]
    return tuple(
        pl.pallas_call(
            functools.partial(kernel, chips, replicas, sections, cap),
            out_shape=[
                jax.ShapeDtypeStruct((2, 1, tokens, width), bf16),
                jax.ShapeDtypeStruct((1, hidden, quarter), bf16),
                jax.ShapeDtypeStruct((1, hidden, quarter), bf16),
            ],
            in_specs=[vmem] * 6 + [anywhere] * 2,
            out_specs=[vmem] * 3,
            scratch_shapes=scratch,
            compiler_params=pltpu.CompilerParams(
                collective_id=0, has_side_effects=True, vmem_limit_bytes=56 * 2**20
            ),
        )(
            in_flight,
            fresh_grads,
            saved_inputs,
            norm_gain,
            expert_ids,
            gate_weights,
            up_weights,
            down_weights,
        )
    )


def solution(mesh):
    in_specs = (
        P("pipe", ("expert", "dp"), None),
        P(None, ("expert", "dp"), None),
        P(None, "pipe", ("expert", "dp"), None),
        P("pipe", None),
        P(None, "pipe", ("expert", "dp"), None),
        P(None, "pipe", ("expert", "dp"), None),
        P("pipe", "expert", None),
        P("pipe", "expert", None),
    )
    out_specs = (
        P(None, "pipe", ("expert", "dp"), None),
        P("pipe", "expert", "dp"),
        P("pipe", "expert", "dp"),
    )
    sizes = tuple(mesh.shape[name] for name in ("pipe", "expert", "dp"))
    return jax.shard_map(
        functools.partial(local, sizes),
        mesh=mesh,
        in_specs=in_specs,
        out_specs=out_specs,
        check_vma=False,
    )
```

```python
import functools

import jax
import jax.numpy as jnp
from jax import lax
from jax.experimental import pallas as pl
from jax.experimental.pallas import tpu as pltpu
from jax.sharding import PartitionSpec as P

norm_eps = 1e-06
MESH = pl.DeviceIdType.MESH
f32 = jnp.float32
bf16 = jnp.bfloat16


def dot(left, right, left_dim, right_dim):
    return lax.dot_general(
        left, right, (((left_dim,), (right_dim,)), ((), ())), preferred_element_type=f32
    )


def kernel(
    chips,
    replicas,
    sections,
    capacity,
    in_flight,
    fresh,
    saved,
    gain,
    ids,
    gates,
    up_hbm,
    down_hbm,
    out_grads,
    out_up,
    out_down,
    up_w,
    down_w,
    select,
    gate_of,
    frames,
    scales,
    snd,
    own,
    sib,
    snd_g,
    own_g,
    sib_g,
    x_all,
    g_all,
    act_all,
    hid_all,
    slope,
    back_sum,
    part_own,
    part_snd,
    part_rcv,
    ret_snd,
    ret_rcv,
    relay_snd,
    relay_rcv,
    far_snd,
    far_rcv,
    near_snd,
    near_rcv,
    kept,
    w_sem,
    disp_s,
    disp_r,
    fwd_s,
    fwd_r,
    part_s,
    part_r,
    ret_s,
    ret_r,
    relay_s,
    relay_r,
    far_s,
    far_r,
    near_s,
    near_r,
):
    n, cap = chips, capacity
    block = 2 * cap
    rows, half = frames.shape[2], frames.shape[3]
    tokens = rows // 2
    per_step = n * block
    quarter = out_up.shape[2]
    place = lax.axis_index("expert")
    chip, core = place // 2, lax.rem(place, 2)
    section = lax.axis_index("pipe")
    replica = lax.axis_index("dp")

    def chip_at(d):
        return {"expert": 2 * lax.rem(chip + d, n) + core}

    sibling = {"expert": 2 * chip + 1 - core}
    section_before = {"pipe": lax.rem(section + sections - 1, sections)}
    section_after = {"pipe": lax.rem(section + 1, sections)}
    replica_after = {"dp": lax.rem(replica + 1, replicas)}
    replica_before = {"dp": lax.rem(replica + replicas - 1, replicas)}

    def remote(src, dst, s_sem, r_sem, to):
        return pltpu.make_async_remote_copy(
            src_ref=src,
            dst_ref=dst,
            send_sem=s_sem,
            recv_sem=r_sem,
            device_id=to,
            device_id_type=MESH,
        )

    load_up = pltpu.make_async_copy(up_hbm.at[0], up_w, w_sem.at[0])
    load_down = pltpu.make_async_copy(down_hbm.at[0], down_w, w_sem.at[1])
    load_up.start()
    load_down.start()

    barrier = pltpu.get_barrier_semaphore()
    partners = [chip_at(d) for d in range(1, n)]
    partners += [sibling, section_before, section_after, replica_after, replica_before]
    for partner in partners:
        pl.semaphore_signal(barrier, inc=1, device_id=partner, device_id_type=MESH)

    def stacked(ref, *at):
        left = ref[(*at, slice(None), slice(0, half))]
        right = ref[(*at, slice(None), slice(half, 2 * half))]
        return jnp.concatenate([left.astype(f32), right.astype(f32)], axis=0)

    gain_row = gain[...].astype(f32)
    gain_two = jnp.concatenate(
        [
            jnp.broadcast_to(gain_row[:, :half], (tokens, half)),
            jnp.broadcast_to(gain_row[:, half:], (tokens, half)),
        ],
        axis=0,
    )

    def feature_mean(values):
        sums = jnp.sum(values, axis=1, keepdims=True)
        both = (sums[:tokens] + sums[tokens:]) * (1.0 / (2 * half))
        return jnp.concatenate([both, both], axis=0)

    def routing(step):
        def as_row(row):
            return jnp.concatenate([row, row], axis=1)

        id_rows = [as_row(ids[step, 0, j : j + 1, :]) for j in range(2)]
        gate_rows = [as_row(gates[step, 0, j : j + 1, :]) for j in range(2)]
        expert = lax.rem(lax.broadcasted_iota(jnp.int32, (n, rows), 0) + chip, n)
        named = [id_rows[j] == expert for j in range(2)]
        member = jnp.where(named[0] | named[1], 1.0, 0.0)
        gate = jnp.where(named[0], gate_rows[0], 0.0) + jnp.where(named[1], gate_rows[1], 0.0)
        r0 = lax.broadcasted_iota(jnp.int32, (rows, rows), 0)
        r1 = lax.broadcasted_iota(jnp.int32, (rows, rows), 1)
        before = (r0 < tokens) & (r0 < lax.rem(r1, tokens))
        slot = dot(member.astype(bf16), jnp.where(before, 1.0, 0.0).astype(bf16), 1, 0)
        at = lax.broadcasted_iota(jnp.int32, (block, rows), 0)
        lane = lax.broadcasted_iota(jnp.int32, (block, rows), 1)
        same_half = (at >= cap) == (lane >= tokens)
        at_slot = jnp.where(at >= cap, at - cap, at).astype(f32)
        for d in range(n):
            hit = same_half & (member[d : d + 1] > 0.5) & (slot[d : d + 1] == at_slot)
            select[step, d * block : (d + 1) * block, :] = jnp.where(hit, 1.0, 0.0).astype(bf16)
            gate_of[step, d * block : (d + 1) * block, :] = jnp.sum(
                jnp.where(hit, gate[d : d + 1], 0.0), axis=1, keepdims=True
            )

    def normed_frames(step):
        inputs = stacked(saved, step, 0)
        scale = lax.rsqrt(feature_mean(inputs * inputs) + norm_eps)
        scales[step] = scale
        return (inputs * scale * gain_two).astype(bf16)

    def held(which, *buffers):
        return [b.at[which] if which < 3 else g.at[which - 3] for b, g in buffers]

    def fill(which, step, values, gated):
        mine, sent = held(which, (own, own_g), (snd, snd_g))
        for d in range(n):
            at = slice(d * block, (d + 1) * block)
            picked = dot(select[step, at, :], values, 1, 0)
            if gated:
                picked = picked * gate_of[step, at, :]
            target = mine.at[0] if d == 0 else sent.at[d]
            target[...] = picked.astype(bf16)

    def dispatch(which, d):
        sent, mine = held(which, (snd, snd_g), (own, own_g))
        return remote(
            sent.at[d], mine.at[d], disp_s.at[which, d], disp_r.at[which, d], chip_at(d)
        )

    def forward(which, d):
        mine, other = held(which, (own, own_g), (sib, sib_g))
        return remote(mine.at[d], other.at[d], fwd_s.at[which, d], fwd_r.at[which, d], sibling)

    groups = [[0, n // 2]] + [[k, n - k] for k in range(n // 2 - 1, 0, -1)]
    last_group = len(groups) - 1
    group_rows = 4 * cap

    def send(which, *among):
        for g in among:
            for d in groups[g]:
                if d != 0:
                    dispatch(which, d).start()

    def receive(which, g):
        for d in groups[g]:
            if d != 0:
                dispatch(which, d).wait_recv()
            forward(which, d).start()

    def unpack(which, g, target, first_row, first_column):
        for side, source in enumerate(held(which, (own, own_g), (sib, sib_g))):
            if side == 1:
                for d in groups[g]:
                    forward(which, d).wait_recv()
            wide = source.shape[-1]
            pieces = [source[d].astype(f32) for d in groups[g]]
            at = first_row + side * 2 * cap
            left = jnp.concatenate([p[:cap] for p in pieces], axis=0)
            right = jnp.concatenate([p[cap:] for p in pieces], axis=0)
            at = slice(at, at + 2 * cap)
            target[at, first_column : first_column + wide] = left.astype(bf16)
            target[at, first_column + wide : first_column + 2 * wide] = right.astype(bf16)

    def take_normed(step, g):
        first = step * per_step + g * group_rows
        unpack(2 * step, g, x_all, first, 0)
        at = slice(first, first + group_rows)
        pre = dot(x_all[at, :], up_w[...], 1, 1)
        sigma = jax.nn.sigmoid(pre)
        act_all[at, :] = (pre * sigma).astype(bf16)
        slope[g * group_rows : (g + 1) * group_rows, :] = sigma * (1.0 + pre * (1.0 - sigma))

    def part_copy(step, g):
        return remote(
            part_snd.at[step, g],
            part_rcv.at[step, g],
            part_s.at[step, g],
            part_r.at[step, g],
            sibling,
        )

    def returning(step, d):
        return remote(
            ret_snd.at[step, d],
            ret_rcv.at[step, d],
            ret_s.at[step, d],
            ret_r.at[step, d],
            chip_at(n - d),
        )

    def finish_part(step, g):
        part_copy(step, g).wait_recv()
        total = part_own[g] + part_rcv[step, g].astype(f32)
        for k, d in enumerate(groups[g]):
            piece = total[k * cap : (k + 1) * cap]
            packed = jnp.concatenate([piece[:, :half], piece[:, half:]], axis=0).astype(bf16)
            if d == 0:
                ret_rcv[step, 0] = packed
            else:
                ret_snd[step, d] = packed
                returning(step, d).start()

    turns = (2, 1, 3, 0)

    def columns_of(k):
        owner = lax.rem(replica + k, replicas)
        return pl.ds(pl.multiple_of(owner * quarter, quarter), quarter)

    def hidden_back(at, j):
        return dot(
            g_all[at, j * quarter : (j + 1) * quarter], down_w[:, columns_of(turns[j])], 1, 1
        )

    def take_grads(step, g):
        first = step * per_step + g * group_rows
        at = slice(first, first + group_rows)
        mine = slice(g * group_rows, (g + 1) * group_rows)
        if step == 0:
            unpack(1, g, g_all, first, 0)
            back = dot(g_all[at, :], down_w[...], 1, 1)
        else:
            unpack(4, g, g_all, first, half)
            back = back_sum[mine, :] + hidden_back(at, 2) + hidden_back(at, 3)
        hidden = (back * slope[mine, :]).astype(bf16)
        hid_all[at, :] = hidden
        part = dot(hidden, up_w[...], 1, 0)
        part_own[g] = part[: 2 * cap]
        part_snd[step, g] = part[2 * cap :].astype(bf16)
        part_copy(step, g).start()

    def finish_step(step, incoming):
        for d in range(1, n):
            returning(step, d).wait_recv()
        back = ret_rcv[step].reshape(n * block, half)
        weighted = gain_two * dot(select[step], back, 0, 0)
        inputs = stacked(saved, step, 0)
        scale = scales[step]
        result = incoming + scale * weighted
        result = result - inputs * (scale * scale * scale) * feature_mean(inputs * weighted)
        result = result.astype(bf16)
        out_grads[step, 0, :, 0:half] = result[:tokens]
        out_grads[step, 0, :, half : 2 * half] = result[tokens:]
        return result

    routing(0)
    fill(0, 0, normed_frames(0), False)
    pl.semaphore_wait(barrier, len(partners))
    send(0, 0, 1)
    frames[0, 0] = stacked(in_flight, 0).astype(bf16)
    fill(1, 0, frames[0, 0], True)
    send(1, 0, 1)
    send(0, 2)
    send(1, 2)
    routing(1)
    fill(2, 1, normed_frames(1), False)

    load_up.wait()
    load_down.wait()
    for g in range(last_group + 1):
        receive(0, g)
        receive(1, g)
        if g + 3 <= last_group:
            send(0, g + 3)
            send(1, g + 3)
        if g > 0:
            finish_part(0, g - 1)
        take_normed(0, g)
        take_grads(0, g)
    finish_part(0, last_group)
    send(2, 0, 1)

    result = finish_step(0, frames[0, 0].astype(f32))
    relay_snd[...] = result
    relay = remote(relay_snd, relay_rcv, relay_s, relay_r, section_before)
    relay.start()
    send(2, 2, 3)
    receive(2, 0)
    take_normed(1, 0)
    relay.wait_recv()
    last = section == sections - 1
    frames[0, 1] = jnp.where(last, stacked(fresh, 0), relay_rcv[...].astype(f32)).astype(bf16)

    def quarter_of(k):
        owner = lax.rem(replica + k, replicas)
        side = pl.multiple_of((owner // 2) * tokens, tokens)
        within = pl.multiple_of(lax.rem(owner, 2) * quarter, quarter)
        return frames[0, 1, pl.ds(side, tokens), pl.ds(within, quarter)]

    for j in range(2):
        pair = [quarter_of(turns[2 * j]), quarter_of(turns[2 * j + 1])]
        fill(3 + j, 1, jnp.concatenate(pair, axis=0), True)
        if j == 0:
            send(3, 0, 1, 2, 3)
    for g in range(1, last_group + 1):
        receive(2, g)
        take_normed(1, g)
    send(4, 0, 1, 2, 3)

    hidden_half = far_snd.shape[2]
    halves = [slice(0, hidden_half), slice(hidden_half, 2 * hidden_half)]
    ways = [replica_after, replica_before]
    down, up = 0, 1

    def slice_of(kind, k):
        if kind == up:
            return dot(hid_all[...], x_all[:, columns_of(k)], 0, 0)
        j = turns.index(k)
        first = dot(act_all[:per_step, :], g_all[:per_step, columns_of(k)], 0, 0)
        return first + dot(
            act_all[per_step:, :], g_all[per_step:, j * quarter : (j + 1) * quarter], 0, 0
        )

    def far(kind, way):
        return remote(
            far_snd.at[kind, way],
            far_rcv.at[kind, way],
            far_s.at[kind, way],
            far_r.at[kind, way],
            ways[way],
        )

    def close(kind, way, part):
        return remote(
            near_snd.at[kind, way, part],
            near_rcv.at[kind, way, part],
            near_s.at[kind, way, part],
            near_r.at[kind, way, part],
            ways[way],
        )

    def send_far(kind):
        value = slice_of(kind, 2)
        for way in range(2):
            far_snd[kind, way] = value[halves[way]].astype(bf16)
            far(kind, way).start()

    def send_near(kind, way):
        value = slice_of(kind, (1, 3)[way])
        near_snd[kind, way, 1 - way] = value[halves[1 - way]].astype(bf16)
        close(kind, way, 1 - way).start()
        kept[kind, way] = value[halves[way]]

    def merge(kind, way):
        far(kind, way).wait_recv()
        near_snd[kind, way, way] = (kept[kind, way] + far_rcv[kind, way].astype(f32)).astype(bf16)
        close(kind, way, way).start()

    def finish_sum(kind, out):
        value = slice_of(kind, 0)
        for part in range(2):
            total = value[halves[part]]
            for way in range(2):
                close(kind, way, part).wait_recv()
                total = total + near_rcv[kind, way, part].astype(f32)
            out[0, halves[part], :] = total.astype(bf16)

    for g in range(last_group + 1):
        receive(3, g)
        if g > 0:
            unpack(3, g - 1, g_all, per_step + (g - 1) * group_rows, 0)
    unpack(3, last_group, g_all, per_step + last_group * group_rows, 0)
    send_far(down)
    send_near(down, 0)
    at = slice(per_step, 2 * per_step)
    back_sum[...] = hidden_back(at, 0) + hidden_back(at, 1)
    receive(4, 0)
    for g in range(last_group + 1):
        if g < last_group:
            receive(4, g + 1)
        take_grads(1, g)
        if g > 0:
            finish_part(1, g - 1)
    send_near(down, 1)
    merge(down, 0)
    send_far(up)
    finish_part(1, last_group)
    merge(down, 1)
    send_near(up, 0)
    send_near(up, 1)
    merge(up, 0)
    merge(up, 1)
    finish_step(1, frames[0, 1].astype(f32))
    finish_sum(down, out_down)
    finish_sum(up, out_up)

    for which in range(5):
        for d in range(n):
            if d != 0:
                dispatch(which, d).wait_send()
            forward(which, d).wait_send()
    for step in range(2):
        for g in range(4):
            part_copy(step, g).wait_send()
        for d in range(1, n):
            returning(step, d).wait_send()
    relay.wait_send()
    for kind in range(2):
        for way in range(2):
            far(kind, way).wait_send()
            for part in range(2):
                close(kind, way, part).wait_send()


def local(
    mesh_sizes,
    in_flight,
    fresh_grads,
    saved_inputs,
    norm_gain,
    expert_ids,
    gate_weights,
    up_weights,
    down_weights,
):
    sections, places, replicas = mesh_sizes
    chips = places // 2
    tokens, width = saved_inputs.shape[2:]
    hidden = up_weights.shape[1]
    cap = min(tokens, 3 * tokens // chips)
    half = width // 2
    block = 2 * cap
    per_step = chips * block
    group_slots = per_step // 8
    quarter = width // replicas
    vmem = pl.BlockSpec(memory_space=pltpu.VMEM)
    anywhere = pl.BlockSpec(memory_space=pl.ANY)
    dma = pltpu.SemaphoreType.DMA
    scratch = [
        pltpu.VMEM((hidden, width), bf16),
        pltpu.VMEM((hidden, width), bf16),
        pltpu.VMEM((2, chips * block, 2 * tokens), bf16),
        pltpu.VMEM((2, chips * block, 1), f32),
        pltpu.VMEM((1, 2, 2 * tokens, half), bf16),
        pltpu.VMEM((2, 2 * tokens, 1), f32),
        pltpu.VMEM((3, chips, block, half), bf16),
        pltpu.VMEM((3, chips, block, half), bf16),
        pltpu.VMEM((3, chips, block, half), bf16),
        pltpu.VMEM((2, chips, block, quarter), bf16),
        pltpu.VMEM((2, chips, block, quarter), bf16),
        pltpu.VMEM((2, chips, block, quarter), bf16),
        pltpu.VMEM((2 * per_step, width), bf16),
        pltpu.VMEM((2 * per_step, width), bf16),
        pltpu.VMEM((2 * per_step, hidden), bf16),
        pltpu.VMEM((2 * per_step, hidden), bf16),
        pltpu.VMEM((per_step, hidden), f32),
        pltpu.VMEM((per_step, hidden), f32),
        pltpu.VMEM((4, group_slots, width), f32),
        pltpu.VMEM((2, 4, group_slots, width), bf16),
        pltpu.VMEM((2, 4, group_slots, width), bf16),
        pltpu.VMEM((2, chips, block, half), bf16),
        pltpu.VMEM((2, chips, block, half), bf16),
        pltpu.VMEM((2 * tokens, half), bf16),
        pltpu.VMEM((2 * tokens, half), bf16),
        pltpu.VMEM((2, 2, hidden // 2, quarter), bf16),
        pltpu.VMEM((2, 2, hidden // 2, quarter), bf16),
        pltpu.VMEM((2, 2, 2, hidden // 2, quarter), bf16),
        pltpu.VMEM((2, 2, 2, hidden // 2, quarter), bf16),
        pltpu.VMEM((2, 2, hidden // 2, quarter), f32),
        dma((2,)),
        dma((5, chips)),
        dma((5, chips)),
        dma((5, chips)),
        dma((5, chips)),
        dma((2, 4)),
        dma((2, 4)),
        dma((2, chips)),
        dma((2, chips)),
        dma,
        dma,
        dma((2, 2)),
        dma((2, 2)),
        dma((2, 2, 2)),
        dma((2, 2, 2)),
    ]
    return tuple(
        pl.pallas_call(
            functools.partial(kernel, chips, replicas, sections, cap),
            out_shape=[
                pltpu.VMEM((2, 1, tokens, width), bf16),
                pltpu.VMEM((1, hidden, quarter), bf16),
                pltpu.VMEM((1, hidden, quarter), bf16),
            ],
            in_specs=[vmem] * 6 + [anywhere] * 2,
            out_specs=[vmem] * 3,
            scratch_shapes=scratch,
            compiler_params=pltpu.CompilerParams(
                collective_id=0, has_side_effects=True, vmem_limit_bytes=56 * 2**20
            ),
        )(
            in_flight,
            fresh_grads,
            saved_inputs,
            norm_gain,
            jnp.swapaxes(expert_ids, 2, 3),
            jnp.swapaxes(gate_weights, 2, 3),
            up_weights,
            down_weights,
        )
    )


def solution(mesh):
    in_specs = (
        P("pipe", ("expert", "dp"), None),
        P(None, ("expert", "dp"), None),
        P(None, "pipe", ("expert", "dp"), None),
        P("pipe", None),
        P(None, "pipe", ("expert", "dp"), None),
        P(None, "pipe", ("expert", "dp"), None),
        P("pipe", "expert", None),
        P("pipe", "expert", None),
    )
    out_specs = (
        P(None, "pipe", ("expert", "dp"), None),
        P("pipe", "expert", "dp"),
        P("pipe", "expert", "dp"),
    )
    sizes = tuple(mesh.shape[name] for name in ("pipe", "expert", "dp"))
    return jax.shard_map(
        functools.partial(local, sizes),
        mesh=mesh,
        in_specs=in_specs,
        out_specs=out_specs,
        check_vma=False,
    )
```

```python
import functools

import jax
import jax.numpy as jnp
from jax import lax
from jax.experimental import pallas as pl
from jax.experimental.pallas import tpu as pltpu
from jax.sharding import PartitionSpec as P

norm_eps = 1e-06
MESH = pl.DeviceIdType.MESH
f32 = jnp.float32
bf16 = jnp.bfloat16


def dot(left, right, left_dim, right_dim):
    return lax.dot_general(
        left, right, (((left_dim,), (right_dim,)), ((), ())), preferred_element_type=f32
    )


def kernel(
    chips,
    replicas,
    sections,
    capacity,
    in_flight_hbm,
    fresh_hbm,
    saved_hbm,
    gain,
    ids,
    gates,
    up_hbm,
    down_hbm,
    out_grads,
    out_up,
    out_down,
    up_w,
    down_w,
    in_flight,
    fresh,
    saved,
    select,
    gate_of,
    frames,
    scales,
    snd,
    own,
    sib,
    snd_g,
    own_g,
    sib_g,
    x_all,
    g_all,
    act_all,
    hid_all,
    slope,
    info_snd,
    info_rcv,
    cols_snd,
    cols_rcv,
    act_oth,
    g_oth,
    part_own,
    part_snd,
    part_rcv,
    ret_snd,
    ret_rcv,
    relay_snd,
    relay_rcv,
    far_snd,
    far_rcv,
    near_snd,
    near_rcv,
    kept,
    w_sem,
    disp_s,
    disp_r,
    fwd_s,
    fwd_r,
    part_s,
    part_r,
    ret_s,
    ret_r,
    relay_s,
    relay_r,
    far_s,
    far_r,
    near_s,
    near_r,
    info_s,
    info_r,
    cols_s,
    cols_r,
    act_s,
    act_r,
):
    n, cap = chips, capacity
    block = 2 * cap
    rows, half = frames.shape[2], frames.shape[3]
    tokens = rows // 2
    per_step = n * block
    quarter = out_up.shape[2]
    place = lax.axis_index("expert")
    chip, core = place // 2, lax.rem(place, 2)
    section = lax.axis_index("pipe")
    replica = lax.axis_index("dp")

    def chip_at(d):
        return {"expert": 2 * lax.rem(chip + d, n) + core}

    sibling = {"expert": 2 * chip + 1 - core}
    section_before = {"pipe": lax.rem(section + sections - 1, sections)}
    section_after = {"pipe": lax.rem(section + 1, sections)}
    replica_after = {"dp": lax.rem(replica + 1, replicas)}
    replica_before = {"dp": lax.rem(replica + replicas - 1, replicas)}
    others = (2, 1, 3)

    def replica_at(k):
        return {"dp": lax.rem(replica + k, replicas)}


    def remote(src, dst, s_sem, r_sem, to):
        return pltpu.make_async_remote_copy(
            src_ref=src,
            dst_ref=dst,
            send_sem=s_sem,
            recv_sem=r_sem,
            device_id=to,
            device_id_type=MESH,
        )

    barrier = pltpu.get_barrier_semaphore()
    partners = [chip_at(d) for d in range(1, n)]
    partners += [sibling, section_before, section_after]
    partners += [replica_at(k) for k in others]
    for partner in partners:
        pl.semaphore_signal(barrier, inc=1, device_id=partner, device_id_type=MESH)

    moves = [
        (saved_hbm.at[0, 0], saved.at[0]),
        (in_flight_hbm.at[0], in_flight),
        (saved_hbm.at[1, 0], saved.at[1]),
        (up_hbm.at[0], up_w),
        (down_hbm.at[0], down_w),
        (fresh_hbm.at[0], fresh),
    ]
    loads = [pltpu.make_async_copy(a, b, w_sem.at[i]) for i, (a, b) in enumerate(moves)]
    for load in loads:
        load.start()

    def stacked(ref, *at):
        left = ref[(*at, slice(None), slice(0, half))]
        right = ref[(*at, slice(None), slice(half, 2 * half))]
        return jnp.concatenate([left.astype(f32), right.astype(f32)], axis=0)

    gain_row = gain[...].astype(f32)
    gain_two = jnp.concatenate(
        [
            jnp.broadcast_to(gain_row[:, :half], (tokens, half)),
            jnp.broadcast_to(gain_row[:, half:], (tokens, half)),
        ],
        axis=0,
    )

    def feature_mean(values):
        sums = jnp.sum(values, axis=1, keepdims=True)
        both = (sums[:tokens] + sums[tokens:]) * (1.0 / (2 * half))
        return jnp.concatenate([both, both], axis=0)

    def as_rows(step):
        both = [
            ids[step, 0].astype(f32),
            gates[step, 0],
        ]
        four = jnp.concatenate(both, axis=0)
        return jnp.concatenate([four, four], axis=1)

    def routing(step, table):
        id_rows = [table[j : j + 1] for j in range(2)]
        gate_rows = [table[2 + j : 3 + j] for j in range(2)]
        expert = lax.rem(lax.broadcasted_iota(jnp.int32, (n, rows), 0) + chip, n).astype(f32)
        named = [id_rows[j] == expert for j in range(2)]
        member = jnp.where(named[0] | named[1], 1.0, 0.0)
        gate = jnp.where(named[0], gate_rows[0], 0.0) + jnp.where(named[1], gate_rows[1], 0.0)
        r0 = lax.broadcasted_iota(jnp.int32, (rows, rows), 0)
        r1 = lax.broadcasted_iota(jnp.int32, (rows, rows), 1)
        before = (r0 < tokens) & (r0 < lax.rem(r1, tokens))
        slot = dot(member.astype(bf16), jnp.where(before, 1.0, 0.0).astype(bf16), 1, 0)
        at = lax.broadcasted_iota(jnp.int32, (block, rows), 0)
        lane = lax.broadcasted_iota(jnp.int32, (block, rows), 1)
        same_half = (at >= cap) == (lane >= tokens)
        at_slot = jnp.where(at >= cap, at - cap, at).astype(f32)
        for d in range(n):
            hit = same_half & (member[d : d + 1] > 0.5) & (slot[d : d + 1] == at_slot)
            select[step, d * block : (d + 1) * block, :] = jnp.where(hit, 1.0, 0.0).astype(bf16)
            gate_of[step, d * block : (d + 1) * block, :] = jnp.sum(
                jnp.where(hit, gate[d : d + 1], 0.0), axis=1, keepdims=True
            )

    def normed_frames(step):
        inputs = stacked(saved, step)
        scale = lax.rsqrt(feature_mean(inputs * inputs) + norm_eps)
        scales[step] = scale
        frames[1, step] = (inputs * scale * gain_two).astype(bf16)

    def held(which, *buffers):
        return [b.at[which] if which < 4 else g.at[which - 4] for b, g in buffers]

    def fill(which, step, values, gated, *among):
        mine, sent = held(which, (own, own_g), (snd, snd_g))
        for d in [d for g in among for d in groups[g]]:
            at = slice(d * block, (d + 1) * block)
            picked = dot(select[step, at, :], values, 1, 0)
            if gated:
                picked = picked * gate_of[step, at, :]
            target = mine.at[0] if d == 0 else sent.at[d]
            target[...] = picked.astype(bf16)

    def dispatch(which, d):
        sent, mine = held(which, (snd, snd_g), (own, own_g))
        return remote(
            sent.at[d], mine.at[d], disp_s.at[which, d], disp_r.at[which, d], chip_at(d)
        )

    def forward(which, d):
        mine, other = held(which, (own, own_g), (sib, sib_g))
        return remote(mine.at[d], other.at[d], fwd_s.at[which, d], fwd_r.at[which, d], sibling)

    groups = [[0, n // 2]] + [[k, n - k] for k in range(n // 2 - 1, 0, -1)]
    last_group = len(groups) - 1
    group_rows = 4 * cap

    def send(which, *among):
        for g in among:
            for d in groups[g]:
                if d != 0:
                    dispatch(which, d).start()

    def receive(which, g):
        for d in groups[g]:
            if d != 0:
                dispatch(which, d).wait_recv()
            forward(which, d).start()

    def unpack(which, g, target, first_row, first_column):
        for side, source in enumerate(held(which, (own, own_g), (sib, sib_g))):
            if side == 1:
                for d in groups[g]:
                    forward(which, d).wait_recv()
            wide = source.shape[-1]
            pieces = [source[d].astype(f32) for d in groups[g]]
            at = first_row + side * 2 * cap
            left = jnp.concatenate([p[:cap] for p in pieces], axis=0)
            right = jnp.concatenate([p[cap:] for p in pieces], axis=0)
            at = slice(at, at + 2 * cap)
            target[at, first_column : first_column + wide] = left.astype(bf16)
            target[at, first_column + wide : first_column + 2 * wide] = right.astype(bf16)

    def take_normed(step, g):
        first = step * per_step + g * group_rows
        unpack(2 * step, g, x_all, first, 0)
        at = slice(first, first + group_rows)
        pre = dot(x_all[at, :], up_w[...], 1, 1)
        sigma = jax.nn.sigmoid(pre)
        act_all[at, :] = (pre * sigma).astype(bf16)
        slope[g * group_rows : (g + 1) * group_rows, :] = sigma * (1.0 + pre * (1.0 - sigma))

    def part_copy(step, g):
        return remote(
            part_snd.at[step, g],
            part_rcv.at[step, g],
            part_s.at[step, g],
            part_r.at[step, g],
            sibling,
        )

    def returning(step, d):
        return remote(
            ret_snd.at[step, d],
            ret_rcv.at[step, d],
            ret_s.at[step, d],
            ret_r.at[step, d],
            chip_at(n - d),
        )

    def finish_part(step, g):
        part_copy(step, g).wait_recv()
        total = part_own[g] + part_rcv[step, g].astype(f32)
        for k, d in enumerate(groups[g]):
            piece = total[k * cap : (k + 1) * cap]
            packed = jnp.concatenate([piece[:, :half], piece[:, half:]], axis=0).astype(bf16)
            if d == 0:
                ret_rcv[step, 0] = packed
            else:
                ret_snd[step, d] = packed
                returning(step, d).start()

    def columns_of(k):
        owner = lax.rem(replica + k, replicas)
        return pl.ds(pl.multiple_of(owner * quarter, quarter), quarter)

    def take_grads(step, g):
        first = step * per_step + g * group_rows
        at = slice(first, first + group_rows)
        mine = slice(g * group_rows, (g + 1) * group_rows)
        unpack(2 * step + 1, g, g_all, first, 0)
        back = dot(g_all[at, :], down_w[...], 1, 1)
        hidden = (back * slope[mine, :]).astype(bf16)
        hid_all[at, :] = hidden
        part = dot(hidden, up_w[...], 1, 0)
        part_own[g] = part[: 2 * cap]
        part_snd[step, g] = part[2 * cap :].astype(bf16)
        part_copy(step, g).start()

    def finish_step(step, incoming):
        for d in range(1, n):
            returning(step, d).wait_recv()
        back = ret_rcv[step].reshape(n * block, half)
        weighted = gain_two * dot(select[step], back, 0, 0)
        inputs = stacked(saved, step)
        scale = scales[step]
        result = incoming + scale * weighted
        result = result - inputs * (scale * scale * scale) * feature_mean(inputs * weighted)
        result = result.astype(bf16)
        out_grads[step, 0, :, 0:half] = result[:tokens]
        out_grads[step, 0, :, half : 2 * half] = result[tokens:]
        return result

    hidden_half = far_snd.shape[2]
    halves = [slice(0, hidden_half), slice(hidden_half, 2 * hidden_half)]
    ways = [replica_after, replica_before]
    down, up = 0, 1

    def slice_of(kind, k):
        if kind == up:
            return dot(hid_all[...], x_all[:, columns_of(k)], 0, 0)
        return dot(act_all[:per_step, :], g_all[:per_step, columns_of(k)], 0, 0)

    def far(kind, way):
        return remote(
            far_snd.at[kind, way],
            far_rcv.at[kind, way],
            far_s.at[kind, way],
            far_r.at[kind, way],
            ways[way],
        )

    def close(kind, way, part):
        return remote(
            near_snd.at[kind, way, part],
            near_rcv.at[kind, way, part],
            near_s.at[kind, way, part],
            near_r.at[kind, way, part],
            ways[way],
        )

    def send_far(kind):
        value = slice_of(kind, 2)
        for way in range(2):
            far_snd[kind, way] = value[halves[way]].astype(bf16)
            far(kind, way).start()

    def send_near(kind, way):
        value = slice_of(kind, (1, 3)[way])
        near_snd[kind, way, 1 - way] = value[halves[1 - way]].astype(bf16)
        close(kind, way, 1 - way).start()
        kept[kind, way] = value[halves[way]]

    def merge(kind, way):
        far(kind, way).wait_recv()
        near_snd[kind, way, way] = (kept[kind, way] + far_rcv[kind, way].astype(f32)).astype(bf16)
        close(kind, way, way).start()

    def info_copy(k):
        return remote(info_snd, info_rcv.at[k - 1], info_s.at[k - 1], info_r.at[k - 1], replica_at(k))

    def cols_copy(k):
        return remote(
            cols_snd.at[k - 1],
            cols_rcv.at[k - 1],
            cols_s.at[k - 1],
            cols_r.at[k - 1],
            replica_at(k),
        )

    def act_copy(way):
        return remote(
            act_all.at[pl.ds(per_step, per_step)],
            act_oth.at[2 * way],
            act_s.at[way],
            act_r.at[way],
            ways[way],
        )

    def act_onward(way):
        part = pl.ds(way * (per_step // 2), per_step // 2)
        return remote(
            act_oth.at[2 * way, part],
            act_oth.at[1, part],
            act_s.at[2 + way],
            act_r.at[2 + way],
            ways[way],
        )

    def later_down():
        value = dot(act_all[per_step:, :], g_all[per_step:, columns_of(0)], 0, 0)
        for way in range(2):
            act_onward(way).wait_recv()
        for k in others:
            first = (k - 1) * per_step
            value = value + dot(act_oth[k - 1], g_oth[first : first + per_step, :], 0, 0)
        return value

    def finish_sum(kind, out):
        value = slice_of(kind, 0)
        if kind == down:
            value = value + later_down()
        for part in range(2):
            total = value[halves[part]]
            for way in range(2):
                close(kind, way, part).wait_recv()
                total = total + near_rcv[kind, way, part].astype(f32)
            out[0, halves[part], :] = total.astype(bf16)

    every = range(last_group + 1)
    routing(0, as_rows(0))
    loads[0].wait()
    normed_frames(0)
    fill(0, 0, frames[1, 0], False, 0, 1)
    pl.semaphore_wait(barrier, len(partners))
    send(0, 0, 1)
    loads[1].wait()
    frames[0, 0] = stacked(in_flight).astype(bf16)
    fill(1, 0, frames[0, 0], True, 0, 1)
    send(1, 0, 1)
    fill(0, 0, frames[1, 0], False, 2, 3)
    fill(1, 0, frames[0, 0], True, 2, 3)
    send(0, 2)
    send(1, 2)
    info_snd[...] = as_rows(1)
    for k in others:
        info_copy(k).start()
    routing(1, info_snd[...])
    loads[2].wait()
    normed_frames(1)
    fill(2, 1, frames[1, 1], False, *every)

    loads[3].wait()
    loads[4].wait()
    for g in range(last_group + 1):
        receive(0, g)
        receive(1, g)
        if g + 3 <= last_group:
            send(0, g + 3)
            send(1, g + 3)
        if g > 0:
            finish_part(0, g - 1)
        take_normed(0, g)
        take_grads(0, g)
    finish_part(0, last_group)
    send(2, 0, 1)
    send_far(down)
    send_near(down, 0)
    send_near(down, 1)
    for k in others:
        info_copy(k).wait_recv()
        routing(1 + k, info_rcv[k - 1])

    result = finish_step(0, frames[0, 0].astype(f32))
    relay_snd[...] = result
    relay = remote(relay_snd, relay_rcv, relay_s, relay_r, section_before)
    relay.start()
    send(2, 2, 3)
    for way in range(2):
        merge(down, way)
    receive(2, 0)
    take_normed(1, 0)
    relay.wait_recv()
    last = section == sections - 1
    loads[5].wait()
    frames[0, 1] = jnp.where(last, stacked(fresh), relay_rcv[...].astype(f32)).astype(bf16)

    def quarter_of(k):
        owner = lax.rem(replica + k, replicas)
        side = pl.multiple_of((owner // 2) * tokens, tokens)
        within = pl.multiple_of(lax.rem(owner, 2) * quarter, quarter)
        return frames[0, 1, pl.ds(side, tokens), pl.ds(within, quarter)]

    fill(3, 1, frames[0, 1], True, *every)
    send(3, 0, 1)
    for k in others:
        whole = quarter_of(k)
        pair = [whole[:, : quarter // 2], whole[:, quarter // 2 :]]
        cols_snd[k - 1] = jnp.concatenate(pair, axis=0)
        cols_copy(k).start()
    for g in every[1:]:
        receive(2, g)
        take_normed(1, g)
        if g == 2:
            send(3, 2)
    send(3, 3)
    for way in range(2):
        act_copy(way).start()
    receive(3, 0)
    for g in every:
        if g < last_group:
            receive(3, g + 1)
        take_grads(1, g)
        if g == last_group - 1:
            for k in others:
                cols_copy(k).wait_recv()
                fill(3 + k, 1 + k, cols_rcv[k - 1], True, *every)
                send(3 + k, *every)
        if g > 0:
            finish_part(1, g - 1)
        if g == last_group - 1:
            for way in range(2):
                act_copy(way).wait_recv()
                act_onward(way).start()
    send_far(up)
    finish_part(1, last_group)
    send_near(up, 0)
    send_near(up, 1)
    merge(up, 0)
    merge(up, 1)
    for k in others:
        for g in every:
            receive(3 + k, g)
    finish_step(1, frames[0, 1].astype(f32))
    for k in others:
        for g in every:
            unpack(3 + k, g, g_oth, (k - 1) * per_step + g * group_rows, 0)
    finish_sum(down, out_down)
    finish_sum(up, out_up)

    for which in range(7):
        for d in range(n):
            if d != 0:
                dispatch(which, d).wait_send()
            forward(which, d).wait_send()
    for step in range(2):
        for g in range(4):
            part_copy(step, g).wait_send()
        for d in range(1, n):
            returning(step, d).wait_send()
    relay.wait_send()
    for k in others:
        info_copy(k).wait_send()
        cols_copy(k).wait_send()
    for way in range(2):
        act_copy(way).wait_send()
        act_onward(way).wait_send()
    for kind in range(2):
        for way in range(2):
            far(kind, way).wait_send()
            for part in range(2):
                close(kind, way, part).wait_send()


def local(
    mesh_sizes,
    in_flight,
    fresh_grads,
    saved_inputs,
    norm_gain,
    expert_ids,
    gate_weights,
    up_weights,
    down_weights,
):
    sections, places, replicas = mesh_sizes
    chips = places // 2
    tokens, width = saved_inputs.shape[2:]
    hidden = up_weights.shape[1]
    cap = min(tokens, 3 * tokens // chips)
    half = width // 2
    block = 2 * cap
    per_step = chips * block
    group_slots = per_step // 8
    quarter = width // replicas
    vmem = pl.BlockSpec(memory_space=pltpu.VMEM)
    anywhere = pl.BlockSpec(memory_space=pl.ANY)
    dma = pltpu.SemaphoreType.DMA
    scratch = [
        pltpu.VMEM((hidden, width), bf16),
        pltpu.VMEM((hidden, width), bf16),
        pltpu.VMEM((tokens, width), bf16),
        pltpu.VMEM((tokens, width), bf16),
        pltpu.VMEM((2, tokens, width), bf16),
        pltpu.VMEM((5, chips * block, 2 * tokens), bf16),
        pltpu.VMEM((5, chips * block, 1), f32),
        pltpu.VMEM((2, 2, 2 * tokens, half), bf16),
        pltpu.VMEM((2, 2 * tokens, 1), f32),
        pltpu.VMEM((4, chips, block, half), bf16),
        pltpu.VMEM((4, chips, block, half), bf16),
        pltpu.VMEM((4, chips, block, half), bf16),
        pltpu.VMEM((3, chips, block, quarter // 2), bf16),
        pltpu.VMEM((3, chips, block, quarter // 2), bf16),
        pltpu.VMEM((3, chips, block, quarter // 2), bf16),
        pltpu.VMEM((2 * per_step, width), bf16),
        pltpu.VMEM((2 * per_step, width), bf16),
        pltpu.VMEM((2 * per_step, hidden), bf16),
        pltpu.VMEM((2 * per_step, hidden), bf16),
        pltpu.VMEM((per_step, hidden), f32),
        pltpu.VMEM((4, 2 * tokens), f32),
        pltpu.VMEM((3, 4, 2 * tokens), f32),
        pltpu.VMEM((3, 2 * tokens, quarter // 2), bf16),
        pltpu.VMEM((3, 2 * tokens, quarter // 2), bf16),
        pltpu.VMEM((3, per_step, hidden), bf16),
        pltpu.VMEM((3 * per_step, quarter), bf16),
        pltpu.VMEM((4, group_slots, width), f32),
        pltpu.VMEM((2, 4, group_slots, width), bf16),
        pltpu.VMEM((2, 4, group_slots, width), bf16),
        pltpu.VMEM((2, chips, block, half), bf16),
        pltpu.VMEM((2, chips, block, half), bf16),
        pltpu.VMEM((2 * tokens, half), bf16),
        pltpu.VMEM((2 * tokens, half), bf16),
        pltpu.VMEM((2, 2, hidden // 2, quarter), bf16),
        pltpu.VMEM((2, 2, hidden // 2, quarter), bf16),
        pltpu.VMEM((2, 2, 2, hidden // 2, quarter), bf16),
        pltpu.VMEM((2, 2, 2, hidden // 2, quarter), bf16),
        pltpu.VMEM((2, 2, hidden // 2, quarter), f32),
        dma((6,)),
        dma((7, chips)),
        dma((7, chips)),
        dma((7, chips)),
        dma((7, chips)),
        dma((2, 4)),
        dma((2, 4)),
        dma((2, chips)),
        dma((2, chips)),
        dma,
        dma,
        dma((2, 2)),
        dma((2, 2)),
        dma((2, 2, 2)),
        dma((2, 2, 2)),
        dma((3,)),
        dma((3,)),
        dma((3,)),
        dma((3,)),
        dma((4,)),
        dma((4,)),
    ]
    return tuple(
        pl.pallas_call(
            functools.partial(kernel, chips, replicas, sections, cap),
            out_shape=[
                pltpu.VMEM((2, 1, tokens, width), bf16),
                pltpu.VMEM((1, hidden, quarter), bf16),
                pltpu.VMEM((1, hidden, quarter), bf16),
            ],
            in_specs=[anywhere] * 3 + [vmem] * 3 + [anywhere] * 2,
            out_specs=[vmem] * 3,
            scratch_shapes=scratch,
            compiler_params=pltpu.CompilerParams(
                collective_id=0, has_side_effects=True, vmem_limit_bytes=56 * 2**20
            ),
        )(
            in_flight,
            fresh_grads,
            saved_inputs,
            norm_gain,
            jnp.swapaxes(expert_ids, 2, 3),
            jnp.swapaxes(gate_weights, 2, 3),
            up_weights,
            down_weights,
        )
    )


def solution(mesh):
    in_specs = (
        P("pipe", ("expert", "dp"), None),
        P(None, ("expert", "dp"), None),
        P(None, "pipe", ("expert", "dp"), None),
        P("pipe", None),
        P(None, "pipe", ("expert", "dp"), None),
        P(None, "pipe", ("expert", "dp"), None),
        P("pipe", "expert", None),
        P("pipe", "expert", None),
    )
    out_specs = (
        P(None, "pipe", ("expert", "dp"), None),
        P("pipe", "expert", "dp"),
        P("pipe", "expert", "dp"),
    )
    sizes = tuple(mesh.shape[name] for name in ("pipe", "expert", "dp"))
    return jax.shard_map(
        functools.partial(local, sizes),
        mesh=mesh,
        in_specs=in_specs,
        out_specs=out_specs,
        check_vma=False,
    )
```

```python
import functools

import jax
import jax.numpy as jnp
from jax import lax
from jax.experimental import pallas as pl
from jax.experimental.pallas import tpu as pltpu
from jax.sharding import PartitionSpec as P

norm_eps = 1e-06
MESH = pl.DeviceIdType.MESH
f32 = jnp.float32
bf16 = jnp.bfloat16


def dot(left, right, left_dim, right_dim):
    return lax.dot_general(
        left, right, (((left_dim,), (right_dim,)), ((), ())), preferred_element_type=f32
    )


def kernel(
    chips,
    replicas,
    sections,
    capacity,
    in_flight_hbm,
    fresh_hbm,
    saved_hbm,
    gain,
    ids,
    gates,
    up_hbm,
    down_hbm,
    out_grads,
    out_up,
    out_down,
    up_w,
    down_w,
    in_flight,
    fresh,
    saved,
    select,
    gate_of,
    frames,
    scales,
    snd,
    own,
    sib,
    snd_g,
    own_g,
    sib_g,
    x_all,
    g_all,
    act_all,
    hid_all,
    slope,
    info_snd,
    info_rcv,
    cols_snd,
    cols_rcv,
    act_oth,
    g_oth,
    part_own,
    part_snd,
    part_rcv,
    ret_snd,
    ret_rcv,
    relay_snd,
    relay_rcv,
    far_snd,
    far_rcv,
    near_snd,
    near_rcv,
    kept,
    w_sem,
    disp_s,
    disp_r,
    fwd_s,
    fwd_r,
    part_s,
    part_r,
    ret_s,
    ret_r,
    relay_s,
    relay_r,
    far_s,
    far_r,
    near_s,
    near_r,
    info_s,
    info_r,
    cols_s,
    cols_r,
    act_s,
    act_r,
):
    n, cap = chips, capacity
    block = 2 * cap
    rows, half = frames.shape[2], frames.shape[3]
    tokens = rows // 2
    per_step = n * block
    quarter = out_up.shape[2]
    place = lax.axis_index("expert")
    chip, core = place // 2, lax.rem(place, 2)
    section = lax.axis_index("pipe")
    replica = lax.axis_index("dp")

    def chip_at(d):
        return {"expert": 2 * lax.rem(chip + d, n) + core}

    sibling = {"expert": 2 * chip + 1 - core}
    section_before = {"pipe": lax.rem(section + sections - 1, sections)}
    section_after = {"pipe": lax.rem(section + 1, sections)}
    replica_after = {"dp": lax.rem(replica + 1, replicas)}
    replica_before = {"dp": lax.rem(replica + replicas - 1, replicas)}
    others = (2, 1, 3)

    def replica_at(k):
        return {"dp": lax.rem(replica + k, replicas)}


    def remote(src, dst, s_sem, r_sem, to):
        return pltpu.make_async_remote_copy(
            src_ref=src,
            dst_ref=dst,
            send_sem=s_sem,
            recv_sem=r_sem,
            device_id=to,
            device_id_type=MESH,
        )

    barrier = pltpu.get_barrier_semaphore()
    partners = [chip_at(d) for d in range(1, n)]
    partners += [sibling, section_before, section_after]
    partners += [replica_at(k) for k in others]
    for partner in partners:
        pl.semaphore_signal(barrier, inc=1, device_id=partner, device_id_type=MESH)

    moves = [
        (saved_hbm.at[0, 0], saved.at[0]),
        (in_flight_hbm.at[0], in_flight),
        (saved_hbm.at[1, 0], saved.at[1]),
        (up_hbm.at[0], up_w),
        (down_hbm.at[0], down_w),
        (fresh_hbm.at[0], fresh),
    ]
    loads = [pltpu.make_async_copy(a, b, w_sem.at[i]) for i, (a, b) in enumerate(moves)]
    for load in loads:
        load.start()

    def stacked(ref, *at):
        left = ref[(*at, slice(None), slice(0, half))]
        right = ref[(*at, slice(None), slice(half, 2 * half))]
        return jnp.concatenate([left.astype(f32), right.astype(f32)], axis=0)

    gain_row = gain[...].astype(f32)
    gain_two = jnp.concatenate(
        [
            jnp.broadcast_to(gain_row[:, :half], (tokens, half)),
            jnp.broadcast_to(gain_row[:, half:], (tokens, half)),
        ],
        axis=0,
    )

    def feature_mean(values):
        sums = jnp.sum(values, axis=1, keepdims=True)
        both = (sums[:tokens] + sums[tokens:]) * (1.0 / (2 * half))
        return jnp.concatenate([both, both], axis=0)

    def as_rows(step):
        both = [
            ids[step, 0].astype(f32),
            gates[step, 0],
        ]
        four = jnp.concatenate(both, axis=0)
        return jnp.concatenate([four, four], axis=1)

    def routing(step, table):
        id_rows = [table[j : j + 1] for j in range(2)]
        gate_rows = [table[2 + j : 3 + j] for j in range(2)]
        expert = lax.rem(lax.broadcasted_iota(jnp.int32, (n, rows), 0) + chip, n).astype(f32)
        named = [id_rows[j] == expert for j in range(2)]
        member = jnp.where(named[0] | named[1], 1.0, 0.0)
        gate = jnp.where(named[0], gate_rows[0], 0.0) + jnp.where(named[1], gate_rows[1], 0.0)
        r0 = lax.broadcasted_iota(jnp.int32, (rows, rows), 0)
        r1 = lax.broadcasted_iota(jnp.int32, (rows, rows), 1)
        before = (r0 < tokens) & (r0 < lax.rem(r1, tokens))
        slot = dot(member.astype(bf16), jnp.where(before, 1.0, 0.0).astype(bf16), 1, 0)
        at = lax.broadcasted_iota(jnp.int32, (block, rows), 0)
        lane = lax.broadcasted_iota(jnp.int32, (block, rows), 1)
        same_half = (at >= cap) == (lane >= tokens)
        at_slot = jnp.where(at >= cap, at - cap, at).astype(f32)
        for d in range(n):
            hit = same_half & (member[d : d + 1] > 0.5) & (slot[d : d + 1] == at_slot)
            select[step, d * block : (d + 1) * block, :] = jnp.where(hit, 1.0, 0.0).astype(bf16)
            gate_of[step, d * block : (d + 1) * block, :] = jnp.sum(
                jnp.where(hit, gate[d : d + 1], 0.0), axis=1, keepdims=True
            )

    def normed_frames(step):
        inputs = stacked(saved, step)
        scale = lax.rsqrt(feature_mean(inputs * inputs) + norm_eps)
        scales[step] = scale
        frames[1, step] = (inputs * scale * gain_two).astype(bf16)

    def held(which, *buffers):
        return [b.at[which] if which < 4 else g.at[which - 4] for b, g in buffers]

    def fill(which, step, values, gated, *among):
        mine, sent = held(which, (own, own_g), (snd, snd_g))
        for d in [d for g in among for d in groups[g]]:
            at = slice(d * block, (d + 1) * block)
            picked = dot(select[step, at, :], values, 1, 0)
            if gated:
                picked = picked * gate_of[step, at, :]
            target = mine.at[0] if d == 0 else sent.at[d]
            target[...] = picked.astype(bf16)

    def dispatch(which, d):
        sent, mine = held(which, (snd, snd_g), (own, own_g))
        return remote(
            sent.at[d], mine.at[d], disp_s.at[which, d], disp_r.at[which, d], chip_at(d)
        )

    def forward(which, d):
        mine, other = held(which, (own, own_g), (sib, sib_g))
        return remote(mine.at[d], other.at[d], fwd_s.at[which, d], fwd_r.at[which, d], sibling)

    groups = [[0, n // 2]] + [[k, n - k] for k in range(n // 2 - 1, 0, -1)]
    last_group = len(groups) - 1
    group_rows = 4 * cap

    def send(which, *among):
        for g in among:
            for d in groups[g]:
                if d != 0:
                    dispatch(which, d).start()

    def receive(which, g):
        for d in groups[g]:
            if d != 0:
                dispatch(which, d).wait_recv()
            forward(which, d).start()

    def unpack(which, g, target, first_row, first_column):
        for side, source in enumerate(held(which, (own, own_g), (sib, sib_g))):
            if side == 1:
                for d in groups[g]:
                    forward(which, d).wait_recv()
            wide = source.shape[-1]
            pieces = [source[d].astype(f32) for d in groups[g]]
            at = first_row + side * 2 * cap
            left = jnp.concatenate([p[:cap] for p in pieces], axis=0)
            right = jnp.concatenate([p[cap:] for p in pieces], axis=0)
            at = slice(at, at + 2 * cap)
            target[at, first_column : first_column + wide] = left.astype(bf16)
            target[at, first_column + wide : first_column + 2 * wide] = right.astype(bf16)

    def take_normed(step, g):
        first = step * per_step + g * group_rows
        unpack(2 * step, g, x_all, first, 0)
        at = slice(first, first + group_rows)
        pre = dot(x_all[at, :], up_w[...], 1, 1)
        sigma = jax.nn.sigmoid(pre)
        act_all[at, :] = (pre * sigma).astype(bf16)
        slope[g * group_rows : (g + 1) * group_rows, :] = sigma * (1.0 + pre * (1.0 - sigma))

    def part_copy(step, g):
        return remote(
            part_snd.at[step, g],
            part_rcv.at[step, g],
            part_s.at[step, g],
            part_r.at[step, g],
            sibling,
        )

    def returning(step, d):
        return remote(
            ret_snd.at[step, d],
            ret_rcv.at[step, d],
            ret_s.at[step, d],
            ret_r.at[step, d],
            chip_at(n - d),
        )

    def finish_part(step, g):
        part_copy(step, g).wait_recv()
        total = part_own[g] + part_rcv[step, g].astype(f32)
        for k, d in enumerate(groups[g]):
            piece = total[k * cap : (k + 1) * cap]
            packed = jnp.concatenate([piece[:, :half], piece[:, half:]], axis=0).astype(bf16)
            if d == 0:
                ret_rcv[step, 0] = packed
            else:
                ret_snd[step, d] = packed
                returning(step, d).start()

    def columns_of(k):
        owner = lax.rem(replica + k, replicas)
        return pl.ds(pl.multiple_of(owner * quarter, quarter), quarter)

    def take_grads(step, g):
        first = step * per_step + g * group_rows
        at = slice(first, first + group_rows)
        mine = slice(g * group_rows, (g + 1) * group_rows)
        unpack(2 * step + 1, g, g_all, first, 0)
        back = dot(g_all[at, :], down_w[...], 1, 1)
        hidden = (back * slope[mine, :]).astype(bf16)
        hid_all[at, :] = hidden
        part = dot(hidden, up_w[...], 1, 0)
        part_own[g] = part[: 2 * cap]
        part_snd[step, g] = part[2 * cap :].astype(bf16)
        part_copy(step, g).start()

    def finish_step(step, incoming):
        for d in range(1, n):
            returning(step, d).wait_recv()
        back = ret_rcv[step].reshape(n * block, half)
        weighted = gain_two * dot(select[step], back, 0, 0)
        inputs = stacked(saved, step)
        scale = scales[step]
        result = incoming + scale * weighted
        result = result - inputs * (scale * scale * scale) * feature_mean(inputs * weighted)
        result = result.astype(bf16)
        out_grads[step, 0, :, 0:half] = result[:tokens]
        out_grads[step, 0, :, half : 2 * half] = result[tokens:]
        return result

    hidden_half = far_snd.shape[2]
    halves = [slice(0, hidden_half), slice(hidden_half, 2 * hidden_half)]
    ways = [replica_after, replica_before]
    down, up = 0, 1

    def slice_of(kind, k):
        if kind == up:
            return dot(hid_all[...], x_all[:, columns_of(k)], 0, 0)
        return dot(act_all[:per_step, :], g_all[:per_step, columns_of(k)], 0, 0)

    def far(kind, way):
        return remote(
            far_snd.at[kind, way],
            far_rcv.at[kind, way],
            far_s.at[kind, way],
            far_r.at[kind, way],
            ways[way],
        )

    def close(kind, way, part):
        return remote(
            near_snd.at[kind, way, part],
            near_rcv.at[kind, way, part],
            near_s.at[kind, way, part],
            near_r.at[kind, way, part],
            ways[way],
        )

    def send_far(kind):
        value = slice_of(kind, 2)
        for way in range(2):
            far_snd[kind, way] = value[halves[way]].astype(bf16)
            far(kind, way).start()

    def send_near(kind, way):
        value = slice_of(kind, (1, 3)[way])
        near_snd[kind, way, 1 - way] = value[halves[1 - way]].astype(bf16)
        close(kind, way, 1 - way).start()
        kept[kind, way] = value[halves[way]]

    def merge(kind, way):
        far(kind, way).wait_recv()
        near_snd[kind, way, way] = (kept[kind, way] + far_rcv[kind, way].astype(f32)).astype(bf16)
        close(kind, way, way).start()

    def info_copy(k):
        return remote(info_snd, info_rcv.at[k - 1], info_s.at[k - 1], info_r.at[k - 1], replica_at(k))

    def cols_copy(k):
        return remote(
            cols_snd.at[k - 1],
            cols_rcv.at[k - 1],
            cols_s.at[k - 1],
            cols_r.at[k - 1],
            replica_at(k),
        )

    def act_copy(way):
        return remote(
            act_all.at[pl.ds(per_step, per_step)],
            act_oth.at[2 * way],
            act_s.at[way],
            act_r.at[way],
            ways[way],
        )

    def act_onward(way):
        part = pl.ds(way * (per_step // 2), per_step // 2)
        return remote(
            act_oth.at[2 * way, part],
            act_oth.at[1, part],
            act_s.at[2 + way],
            act_r.at[2 + way],
            ways[way],
        )

    def later_down():
        value = dot(act_all[per_step:, :], g_all[per_step:, columns_of(0)], 0, 0)
        for way in range(2):
            act_onward(way).wait_recv()
        for k in others:
            first = (k - 1) * per_step
            value = value + dot(act_oth[k - 1], g_oth[first : first + per_step, :], 0, 0)
        return value

    def finish_sum(kind, out):
        value = slice_of(kind, 0)
        if kind == down:
            value = value + later_down()
        for part in range(2):
            total = value[halves[part]]
            for way in range(2):
                close(kind, way, part).wait_recv()
                total = total + near_rcv[kind, way, part].astype(f32)
            out[0, halves[part], :] = total.astype(bf16)

    every = range(last_group + 1)
    routing(0, as_rows(0))
    loads[0].wait()
    normed_frames(0)
    fill(0, 0, frames[1, 0], False, 0, 1)
    pl.semaphore_wait(barrier, len(partners))
    send(0, 0, 1)
    loads[1].wait()
    frames[0, 0] = stacked(in_flight).astype(bf16)
    fill(1, 0, frames[0, 0], True, 0, 1)
    send(1, 0, 1)
    fill(0, 0, frames[1, 0], False, 2, 3)
    fill(1, 0, frames[0, 0], True, 2, 3)
    send(0, 2)
    send(1, 2)
    info_snd[...] = as_rows(1)
    for k in others:
        info_copy(k).start()
    routing(1, info_snd[...])
    loads[2].wait()
    normed_frames(1)
    fill(2, 1, frames[1, 1], False, *every)

    loads[3].wait()
    loads[4].wait()
    for g in range(last_group + 1):
        receive(0, g)
        receive(1, g)
        if g + 3 <= last_group:
            send(0, g + 3)
            send(1, g + 3)
        if g > 0:
            finish_part(0, g - 1)
        take_normed(0, g)
        take_grads(0, g)
    finish_part(0, last_group)
    send(2, 0, 1)
    send_far(down)
    send_near(down, 0)
    send_near(down, 1)
    for k in others:
        info_copy(k).wait_recv()
        routing(1 + k, info_rcv[k - 1])

    result = finish_step(0, frames[0, 0].astype(f32))
    relay_snd[...] = result
    relay = remote(relay_snd, relay_rcv, relay_s, relay_r, section_before)
    pl.when(section > 0)(relay.start)
    send(2, 2, 3)
    for way in range(2):
        merge(down, way)
    receive(2, 0)
    take_normed(1, 0)
    pl.when(section < sections - 1)(relay.wait_recv)
    loads[5].wait()

    @pl.when(section == sections - 1)
    def _():
        relay_rcv[...] = stacked(fresh).astype(bf16)

    frames[0, 1] = relay_rcv[...]

    def quarter_of(k):
        owner = lax.rem(replica + k, replicas)
        side = pl.multiple_of((owner // 2) * tokens, tokens)
        within = pl.multiple_of(lax.rem(owner, 2) * quarter, quarter)
        return frames[0, 1, pl.ds(side, tokens), pl.ds(within, quarter)]

    fill(3, 1, frames[0, 1], True, *every)
    send(3, 0, 1)
    for k in others:
        whole = quarter_of(k)
        pair = [whole[:, : quarter // 2], whole[:, quarter // 2 :]]
        cols_snd[k - 1] = jnp.concatenate(pair, axis=0)
        cols_copy(k).start()
    for g in every[1:]:
        receive(2, g)
        take_normed(1, g)
        if g == 2:
            send(3, 2)
    send(3, 3)
    for way in range(2):
        act_copy(way).start()
    receive(3, 0)
    for g in every:
        if g < last_group:
            receive(3, g + 1)
        take_grads(1, g)
        if g == last_group - 1:
            for k in others:
                cols_copy(k).wait_recv()
                fill(3 + k, 1 + k, cols_rcv[k - 1], True, *every)
                send(3 + k, *every)
        if g > 0:
            finish_part(1, g - 1)
        if g == last_group - 1:
            for way in range(2):
                act_copy(way).wait_recv()
                act_onward(way).start()
    send_far(up)
    finish_part(1, last_group)
    send_near(up, 0)
    send_near(up, 1)
    merge(up, 0)
    merge(up, 1)
    for k in others:
        for g in every:
            receive(3 + k, g)
    finish_step(1, frames[0, 1].astype(f32))
    for k in others:
        for g in every:
            unpack(3 + k, g, g_oth, (k - 1) * per_step + g * group_rows, 0)
    finish_sum(down, out_down)
    finish_sum(up, out_up)

    for which in range(7):
        for d in range(n):
            if d != 0:
                dispatch(which, d).wait_send()
            forward(which, d).wait_send()
    for step in range(2):
        for g in range(4):
            part_copy(step, g).wait_send()
        for d in range(1, n):
            returning(step, d).wait_send()
    pl.when(section > 0)(relay.wait_send)
    for k in others:
        info_copy(k).wait_send()
        cols_copy(k).wait_send()
    for way in range(2):
        act_copy(way).wait_send()
        act_onward(way).wait_send()
    for kind in range(2):
        for way in range(2):
            far(kind, way).wait_send()
            for part in range(2):
                close(kind, way, part).wait_send()


def local(
    mesh_sizes,
    in_flight,
    fresh_grads,
    saved_inputs,
    norm_gain,
    expert_ids,
    gate_weights,
    up_weights,
    down_weights,
):
    sections, places, replicas = mesh_sizes
    chips = places // 2
    tokens, width = saved_inputs.shape[2:]
    hidden = up_weights.shape[1]
    cap = min(tokens, 3 * tokens // chips)
    half = width // 2
    block = 2 * cap
    per_step = chips * block
    group_slots = per_step // 8
    quarter = width // replicas
    vmem = pl.BlockSpec(memory_space=pltpu.VMEM)
    anywhere = pl.BlockSpec(memory_space=pl.ANY)
    dma = pltpu.SemaphoreType.DMA
    scratch = [
        pltpu.VMEM((hidden, width), bf16),
        pltpu.VMEM((hidden, width), bf16),
        pltpu.VMEM((tokens, width), bf16),
        pltpu.VMEM((tokens, width), bf16),
        pltpu.VMEM((2, tokens, width), bf16),
        pltpu.VMEM((5, chips * block, 2 * tokens), bf16),
        pltpu.VMEM((5, chips * block, 1), f32),
        pltpu.VMEM((2, 2, 2 * tokens, half), bf16),
        pltpu.VMEM((2, 2 * tokens, 1), f32),
        pltpu.VMEM((4, chips, block, half), bf16),
        pltpu.VMEM((4, chips, block, half), bf16),
        pltpu.VMEM((4, chips, block, half), bf16),
        pltpu.VMEM((3, chips, block, quarter // 2), bf16),
        pltpu.VMEM((3, chips, block, quarter // 2), bf16),
        pltpu.VMEM((3, chips, block, quarter // 2), bf16),
        pltpu.VMEM((2 * per_step, width), bf16),
        pltpu.VMEM((2 * per_step, width), bf16),
        pltpu.VMEM((2 * per_step, hidden), bf16),
        pltpu.VMEM((2 * per_step, hidden), bf16),
        pltpu.VMEM((per_step, hidden), f32),
        pltpu.VMEM((4, 2 * tokens), f32),
        pltpu.VMEM((3, 4, 2 * tokens), f32),
        pltpu.VMEM((3, 2 * tokens, quarter // 2), bf16),
        pltpu.VMEM((3, 2 * tokens, quarter // 2), bf16),
        pltpu.VMEM((3, per_step, hidden), bf16),
        pltpu.VMEM((3 * per_step, quarter), bf16),
        pltpu.VMEM((4, group_slots, width), f32),
        pltpu.VMEM((2, 4, group_slots, width), bf16),
        pltpu.VMEM((2, 4, group_slots, width), bf16),
        pltpu.VMEM((2, chips, block, half), bf16),
        pltpu.VMEM((2, chips, block, half), bf16),
        pltpu.VMEM((2 * tokens, half), bf16),
        pltpu.VMEM((2 * tokens, half), bf16),
        pltpu.VMEM((2, 2, hidden // 2, quarter), bf16),
        pltpu.VMEM((2, 2, hidden // 2, quarter), bf16),
        pltpu.VMEM((2, 2, 2, hidden // 2, quarter), bf16),
        pltpu.VMEM((2, 2, 2, hidden // 2, quarter), bf16),
        pltpu.VMEM((2, 2, hidden // 2, quarter), f32),
        dma((6,)),
        dma((7, chips)),
        dma((7, chips)),
        dma((7, chips)),
        dma((7, chips)),
        dma((2, 4)),
        dma((2, 4)),
        dma((2, chips)),
        dma((2, chips)),
        dma,
        dma,
        dma((2, 2)),
        dma((2, 2)),
        dma((2, 2, 2)),
        dma((2, 2, 2)),
        dma((3,)),
        dma((3,)),
        dma((3,)),
        dma((3,)),
        dma((4,)),
        dma((4,)),
    ]
    return tuple(
        pl.pallas_call(
            functools.partial(kernel, chips, replicas, sections, cap),
            out_shape=[
                pltpu.VMEM((2, 1, tokens, width), bf16),
                pltpu.VMEM((1, hidden, quarter), bf16),
                pltpu.VMEM((1, hidden, quarter), bf16),
            ],
            in_specs=[anywhere] * 3 + [vmem] * 3 + [anywhere] * 2,
            out_specs=[vmem] * 3,
            scratch_shapes=scratch,
            compiler_params=pltpu.CompilerParams(
                collective_id=0, has_side_effects=True, vmem_limit_bytes=56 * 2**20
            ),
        )(
            in_flight,
            fresh_grads,
            saved_inputs,
            norm_gain,
            jnp.swapaxes(expert_ids, 2, 3),
            jnp.swapaxes(gate_weights, 2, 3),
            up_weights,
            down_weights,
        )
    )


def solution(mesh):
    in_specs = (
        P("pipe", ("expert", "dp"), None),
        P(None, ("expert", "dp"), None),
        P(None, "pipe", ("expert", "dp"), None),
        P("pipe", None),
        P(None, "pipe", ("expert", "dp"), None),
        P(None, "pipe", ("expert", "dp"), None),
        P("pipe", "expert", None),
        P("pipe", "expert", None),
    )
    out_specs = (
        P(None, "pipe", ("expert", "dp"), None),
        P("pipe", "expert", "dp"),
        P("pipe", "expert", "dp"),
    )
    sizes = tuple(mesh.shape[name] for name in ("pipe", "expert", "dp"))
    return jax.shard_map(
        functools.partial(local, sizes),
        mesh=mesh,
        in_specs=in_specs,
        out_specs=out_specs,
        check_vma=False,
    )
```

```python
import functools

import jax
import jax.numpy as jnp
from jax import lax
from jax.experimental import pallas as pl
from jax.experimental.pallas import tpu as pltpu
from jax.sharding import PartitionSpec as P

norm_eps = 1e-06
MESH = pl.DeviceIdType.MESH
f32 = jnp.float32
bf16 = jnp.bfloat16


def dot(left, right, left_dim, right_dim):
    return lax.dot_general(
        left, right, (((left_dim,), (right_dim,)), ((), ())), preferred_element_type=f32
    )


def kernel(
    chips,
    replicas,
    sections,
    capacity,
    in_flight_hbm,
    fresh_hbm,
    saved_hbm,
    gain_hbm,
    ids_hbm,
    gates_hbm,
    up_hbm,
    down_hbm,
    out_grads,
    out_up,
    out_down,
    up_w,
    down_w,
    in_flight,
    fresh,
    saved,
    gain,
    ids,
    gates,
    select,
    gate_of,
    frames,
    scales,
    snd,
    own,
    sib,
    snd_g,
    own_g,
    sib_g,
    x_all,
    g_all,
    act_all,
    hid_all,
    slope,
    info_snd,
    info_rcv,
    cols_snd,
    cols_rcv,
    act_oth,
    g_oth,
    part_own,
    part_snd,
    part_rcv,
    ret_snd,
    ret_rcv,
    relay_snd,
    relay_rcv,
    far_snd,
    far_rcv,
    near_snd,
    near_rcv,
    kept,
    w_sem,
    disp_s,
    disp_r,
    fwd_s,
    fwd_r,
    part_s,
    part_r,
    ret_s,
    ret_r,
    relay_s,
    relay_r,
    far_s,
    far_r,
    near_s,
    near_r,
    info_s,
    info_r,
    cols_s,
    cols_r,
    act_s,
    act_r,
):
    n, cap = chips, capacity
    block = 2 * cap
    rows, half = frames.shape[2], frames.shape[3]
    tokens = rows // 2
    per_step = n * block
    quarter = out_up.shape[2]
    place = lax.axis_index("expert")
    chip, core = place // 2, lax.rem(place, 2)
    section = lax.axis_index("pipe")
    replica = lax.axis_index("dp")

    def chip_at(d):
        return {"expert": 2 * lax.rem(chip + d, n) + core}

    sibling = {"expert": 2 * chip + 1 - core}
    section_before = {"pipe": lax.rem(section + sections - 1, sections)}
    section_after = {"pipe": lax.rem(section + 1, sections)}
    replica_after = {"dp": lax.rem(replica + 1, replicas)}
    replica_before = {"dp": lax.rem(replica + replicas - 1, replicas)}
    others = (2, 1, 3)

    def replica_at(k):
        return {"dp": lax.rem(replica + k, replicas)}


    def remote(src, dst, s_sem, r_sem, to):
        return pltpu.make_async_remote_copy(
            src_ref=src,
            dst_ref=dst,
            send_sem=s_sem,
            recv_sem=r_sem,
            device_id=to,
            device_id_type=MESH,
        )

    barrier = pltpu.get_barrier_semaphore()
    partners = [chip_at(d) for d in range(1, n)]
    partners += [sibling, section_before, section_after]
    partners += [replica_at(k) for k in others]
    for partner in partners:
        pl.semaphore_signal(barrier, inc=1, device_id=partner, device_id_type=MESH)

    moves = [
        (saved_hbm.at[0, 0], saved.at[0]),
        (in_flight_hbm.at[0], in_flight),
        (saved_hbm.at[1, 0], saved.at[1]),
        (up_hbm.at[0], up_w),
        (down_hbm.at[0], down_w),
        (fresh_hbm.at[0], fresh),
        (ids_hbm, ids),
        (gates_hbm, gates),
        (gain_hbm, gain),
    ]
    loads = [pltpu.make_async_copy(a, b, w_sem.at[i]) for i, (a, b) in enumerate(moves)]
    for load in loads[6:] + loads[:6]:
        load.start()
    for load in loads[6:]:
        load.wait()

    def stacked(ref, *at):
        left = ref[(*at, slice(None), slice(0, half))]
        right = ref[(*at, slice(None), slice(half, 2 * half))]
        return jnp.concatenate([left.astype(f32), right.astype(f32)], axis=0)

    gain_row = gain[...].astype(f32)
    gain_two = jnp.concatenate(
        [
            jnp.broadcast_to(gain_row[:, :half], (tokens, half)),
            jnp.broadcast_to(gain_row[:, half:], (tokens, half)),
        ],
        axis=0,
    )

    def feature_mean(values):
        sums = jnp.sum(values, axis=1, keepdims=True)
        both = (sums[:tokens] + sums[tokens:]) * (1.0 / (2 * half))
        return jnp.concatenate([both, both], axis=0)

    def as_rows(step):
        both = [
            ids[step, 0].astype(f32),
            gates[step, 0],
        ]
        four = jnp.concatenate(both, axis=0)
        return jnp.concatenate([four, four], axis=1)

    def routing(step, table):
        id_rows = [table[j : j + 1] for j in range(2)]
        gate_rows = [table[2 + j : 3 + j] for j in range(2)]
        expert = lax.rem(lax.broadcasted_iota(jnp.int32, (n, rows), 0) + chip, n).astype(f32)
        named = [id_rows[j] == expert for j in range(2)]
        member = jnp.where(named[0] | named[1], 1.0, 0.0)
        gate = jnp.where(named[0], gate_rows[0], 0.0) + jnp.where(named[1], gate_rows[1], 0.0)
        r0 = lax.broadcasted_iota(jnp.int32, (rows, rows), 0)
        r1 = lax.broadcasted_iota(jnp.int32, (rows, rows), 1)
        before = (r0 < tokens) & (r0 < lax.rem(r1, tokens))
        slot = dot(member.astype(bf16), jnp.where(before, 1.0, 0.0).astype(bf16), 1, 0)
        at = lax.broadcasted_iota(jnp.int32, (block, rows), 0)
        lane = lax.broadcasted_iota(jnp.int32, (block, rows), 1)
        same_half = (at >= cap) == (lane >= tokens)
        at_slot = jnp.where(at >= cap, at - cap, at).astype(f32)
        for d in range(n):
            hit = same_half & (member[d : d + 1] > 0.5) & (slot[d : d + 1] == at_slot)
            select[step, d * block : (d + 1) * block, :] = jnp.where(hit, 1.0, 0.0).astype(bf16)
            gate_of[step, d * block : (d + 1) * block, :] = jnp.sum(
                jnp.where(hit, gate[d : d + 1], 0.0), axis=1, keepdims=True
            )

    def normed_frames(step):
        inputs = stacked(saved, step)
        scale = lax.rsqrt(feature_mean(inputs * inputs) + norm_eps)
        scales[step] = scale
        frames[1, step] = (inputs * scale * gain_two).astype(bf16)

    def held(which, *buffers):
        return [b.at[which] if which < 4 else g.at[which - 4] for b, g in buffers]

    def fill(which, step, values, gated, *among):
        mine, sent = held(which, (own, own_g), (snd, snd_g))
        for d in [d for g in among for d in groups[g]]:
            at = slice(d * block, (d + 1) * block)
            picked = dot(select[step, at, :], values, 1, 0)
            if gated:
                picked = picked * gate_of[step, at, :]
            target = mine.at[0] if d == 0 else sent.at[d]
            target[...] = picked.astype(bf16)

    def dispatch(which, d):
        sent, mine = held(which, (snd, snd_g), (own, own_g))
        return remote(
            sent.at[d], mine.at[d], disp_s.at[which, d], disp_r.at[which, d], chip_at(d)
        )

    def forward(which, d):
        mine, other = held(which, (own, own_g), (sib, sib_g))
        return remote(mine.at[d], other.at[d], fwd_s.at[which, d], fwd_r.at[which, d], sibling)

    groups = [[0, n // 2]] + [[k, n - k] for k in range(n // 2 - 1, 0, -1)]
    last_group = len(groups) - 1
    group_rows = 4 * cap

    def send(which, *among):
        for g in among:
            for d in groups[g]:
                if d != 0:
                    dispatch(which, d).start()

    def receive(which, g):
        for d in groups[g]:
            if d != 0:
                dispatch(which, d).wait_recv()
            forward(which, d).start()

    def unpack(which, g, target, first_row, first_column):
        for side, source in enumerate(held(which, (own, own_g), (sib, sib_g))):
            if side == 1:
                for d in groups[g]:
                    forward(which, d).wait_recv()
            wide = source.shape[-1]
            pieces = [source[d].astype(f32) for d in groups[g]]
            at = first_row + side * 2 * cap
            left = jnp.concatenate([p[:cap] for p in pieces], axis=0)
            right = jnp.concatenate([p[cap:] for p in pieces], axis=0)
            at = slice(at, at + 2 * cap)
            target[at, first_column : first_column + wide] = left.astype(bf16)
            target[at, first_column + wide : first_column + 2 * wide] = right.astype(bf16)

    def take_normed(step, g):
        first = step * per_step + g * group_rows
        unpack(2 * step, g, x_all, first, 0)
        at = slice(first, first + group_rows)
        pre = dot(x_all[at, :], up_w[...], 1, 1)
        sigma = jax.nn.sigmoid(pre)
        act_all[at, :] = (pre * sigma).astype(bf16)
        slope[g * group_rows : (g + 1) * group_rows, :] = sigma * (1.0 + pre * (1.0 - sigma))

    def part_copy(step, g):
        return remote(
            part_snd.at[step, g],
            part_rcv.at[step, g],
            part_s.at[step, g],
            part_r.at[step, g],
            sibling,
        )

    def returning(step, d):
        return remote(
            ret_snd.at[step, d],
            ret_rcv.at[step, d],
            ret_s.at[step, d],
            ret_r.at[step, d],
            chip_at(n - d),
        )

    def finish_part(step, g):
        part_copy(step, g).wait_recv()
        total = part_own[g] + part_rcv[step, g].astype(f32)
        for k, d in enumerate(groups[g]):
            piece = total[k * cap : (k + 1) * cap]
            packed = jnp.concatenate([piece[:, :half], piece[:, half:]], axis=0).astype(bf16)
            if d == 0:
                ret_rcv[step, 0] = packed
            else:
                ret_snd[step, d] = packed
                returning(step, d).start()

    def columns_of(k):
        owner = lax.rem(replica + k, replicas)
        return pl.ds(pl.multiple_of(owner * quarter, quarter), quarter)

    def take_grads(step, g):
        first = step * per_step + g * group_rows
        at = slice(first, first + group_rows)
        mine = slice(g * group_rows, (g + 1) * group_rows)
        unpack(2 * step + 1, g, g_all, first, 0)
        back = dot(g_all[at, :], down_w[...], 1, 1)
        hidden = (back * slope[mine, :]).astype(bf16)
        hid_all[at, :] = hidden
        part = dot(hidden, up_w[...], 1, 0)
        part_own[g] = part[: 2 * cap]
        part_snd[step, g] = part[2 * cap :].astype(bf16)
        part_copy(step, g).start()

    def finish_step(step, incoming):
        for d in range(1, n):
            returning(step, d).wait_recv()
        back = ret_rcv[step].reshape(n * block, half)
        weighted = gain_two * dot(select[step], back, 0, 0)
        inputs = stacked(saved, step)
        scale = scales[step]
        result = incoming + scale * weighted
        result = result - inputs * (scale * scale * scale) * feature_mean(inputs * weighted)
        result = result.astype(bf16)
        out_grads[step, 0, :, 0:half] = result[:tokens]
        out_grads[step, 0, :, half : 2 * half] = result[tokens:]
        return result

    hidden_half = far_snd.shape[2]
    halves = [slice(0, hidden_half), slice(hidden_half, 2 * hidden_half)]
    ways = [replica_after, replica_before]
    down, up = 0, 1

    def slice_of(kind, k):
        if kind == up:
            return dot(hid_all[...], x_all[:, columns_of(k)], 0, 0)
        return dot(act_all[:per_step, :], g_all[:per_step, columns_of(k)], 0, 0)

    def far(kind, way):
        return remote(
            far_snd.at[kind, way],
            far_rcv.at[kind, way],
            far_s.at[kind, way],
            far_r.at[kind, way],
            ways[way],
        )

    def close(kind, way, part):
        return remote(
            near_snd.at[kind, way, part],
            near_rcv.at[kind, way, part],
            near_s.at[kind, way, part],
            near_r.at[kind, way, part],
            ways[way],
        )

    def send_far(kind):
        value = slice_of(kind, 2)
        for way in range(2):
            far_snd[kind, way] = value[halves[way]].astype(bf16)
            far(kind, way).start()

    def send_near(kind, way):
        value = slice_of(kind, (1, 3)[way])
        near_snd[kind, way, 1 - way] = value[halves[1 - way]].astype(bf16)
        close(kind, way, 1 - way).start()
        kept[kind, way] = value[halves[way]]

    def merge(kind, way):
        far(kind, way).wait_recv()
        near_snd[kind, way, way] = (kept[kind, way] + far_rcv[kind, way].astype(f32)).astype(bf16)
        close(kind, way, way).start()

    def info_copy(k):
        return remote(info_snd, info_rcv.at[k - 1], info_s.at[k - 1], info_r.at[k - 1], replica_at(k))

    def cols_copy(k):
        return remote(
            cols_snd.at[k - 1],
            cols_rcv.at[k - 1],
            cols_s.at[k - 1],
            cols_r.at[k - 1],
            replica_at(k),
        )

    def act_copy(way):
        return remote(
            act_all.at[pl.ds(per_step, per_step)],
            act_oth.at[2 * way],
            act_s.at[way],
            act_r.at[way],
            ways[way],
        )

    def act_onward(way):
        part = pl.ds(way * (per_step // 2), per_step // 2)
        return remote(
            act_oth.at[2 * way, part],
            act_oth.at[1, part],
            act_s.at[2 + way],
            act_r.at[2 + way],
            ways[way],
        )

    def later_down():
        value = dot(act_all[per_step:, :], g_all[per_step:, columns_of(0)], 0, 0)
        for way in range(2):
            act_onward(way).wait_recv()
        for k in others:
            first = (k - 1) * per_step
            value = value + dot(act_oth[k - 1], g_oth[first : first + per_step, :], 0, 0)
        return value

    def finish_sum(kind, out):
        value = slice_of(kind, 0)
        if kind == down:
            value = value + later_down()
        for part in range(2):
            total = value[halves[part]]
            for way in range(2):
                close(kind, way, part).wait_recv()
                total = total + near_rcv[kind, way, part].astype(f32)
            out[0, halves[part], :] = total.astype(bf16)

    every = range(last_group + 1)
    routing(0, as_rows(0))
    loads[0].wait()
    normed_frames(0)
    fill(0, 0, frames[1, 0], False, 0, 1)
    pl.semaphore_wait(barrier, len(partners))
    send(0, 0, 1)
    loads[1].wait()
    frames[0, 0] = stacked(in_flight).astype(bf16)
    fill(1, 0, frames[0, 0], True, 0, 1)
    send(1, 0, 1)
    fill(0, 0, frames[1, 0], False, 2, 3)
    fill(1, 0, frames[0, 0], True, 2, 3)
    send(0, 2)
    send(1, 2)
    info_snd[...] = as_rows(1)
    for k in others:
        info_copy(k).start()
    routing(1, info_snd[...])
    loads[2].wait()
    normed_frames(1)
    fill(2, 1, frames[1, 1], False, *every)

    loads[3].wait()
    loads[4].wait()
    for g in range(last_group + 1):
        receive(0, g)
        receive(1, g)
        if g + 3 <= last_group:
            send(0, g + 3)
            send(1, g + 3)
        if g > 0:
            finish_part(0, g - 1)
        take_normed(0, g)
        take_grads(0, g)
    finish_part(0, last_group)
    send(2, 0, 1)
    send_far(down)
    send_near(down, 0)
    send_near(down, 1)
    for k in others:
        info_copy(k).wait_recv()
        routing(1 + k, info_rcv[k - 1])

    result = finish_step(0, frames[0, 0].astype(f32))
    relay_snd[...] = result
    relay = remote(relay_snd, relay_rcv, relay_s, relay_r, section_before)
    pl.when(section > 0)(relay.start)
    send(2, 2, 3)
    for way in range(2):
        merge(down, way)
    receive(2, 0)
    take_normed(1, 0)
    pl.when(section < sections - 1)(relay.wait_recv)
    loads[5].wait()

    @pl.when(section == sections - 1)
    def _():
        relay_rcv[...] = stacked(fresh).astype(bf16)

    frames[0, 1] = relay_rcv[...]

    def quarter_of(k):
        owner = lax.rem(replica + k, replicas)
        side = pl.multiple_of((owner // 2) * tokens, tokens)
        within = pl.multiple_of(lax.rem(owner, 2) * quarter, quarter)
        return frames[0, 1, pl.ds(side, tokens), pl.ds(within, quarter)]

    fill(3, 1, frames[0, 1], True, *every)
    send(3, 0, 1)
    for k in others:
        whole = quarter_of(k)
        pair = [whole[:, : quarter // 2], whole[:, quarter // 2 :]]
        cols_snd[k - 1] = jnp.concatenate(pair, axis=0)
        cols_copy(k).start()
    for g in every[1:]:
        receive(2, g)
        take_normed(1, g)
        if g == 2:
            send(3, 2)
    send(3, 3)
    for way in range(2):
        act_copy(way).start()
    receive(3, 0)
    for g in every:
        if g < last_group:
            receive(3, g + 1)
        take_grads(1, g)
        if g == last_group - 1:
            for k in others:
                cols_copy(k).wait_recv()
                fill(3 + k, 1 + k, cols_rcv[k - 1], True, *every)
                send(3 + k, *every)
        if g > 0:
            finish_part(1, g - 1)
        if g == last_group - 1:
            for way in range(2):
                act_copy(way).wait_recv()
                act_onward(way).start()
    send_far(up)
    finish_part(1, last_group)
    send_near(up, 0)
    send_near(up, 1)
    merge(up, 0)
    merge(up, 1)
    for k in others:
        for g in every:
            receive(3 + k, g)
    finish_step(1, frames[0, 1].astype(f32))
    for k in others:
        for g in every:
            unpack(3 + k, g, g_oth, (k - 1) * per_step + g * group_rows, 0)
    finish_sum(down, out_down)
    finish_sum(up, out_up)

    for which in range(7):
        for d in range(n):
            if d != 0:
                dispatch(which, d).wait_send()
            forward(which, d).wait_send()
    for step in range(2):
        for g in range(4):
            part_copy(step, g).wait_send()
        for d in range(1, n):
            returning(step, d).wait_send()
    pl.when(section > 0)(relay.wait_send)
    for k in others:
        info_copy(k).wait_send()
        cols_copy(k).wait_send()
    for way in range(2):
        act_copy(way).wait_send()
        act_onward(way).wait_send()
    for kind in range(2):
        for way in range(2):
            far(kind, way).wait_send()
            for part in range(2):
                close(kind, way, part).wait_send()


def local(
    mesh_sizes,
    in_flight,
    fresh_grads,
    saved_inputs,
    norm_gain,
    expert_ids,
    gate_weights,
    up_weights,
    down_weights,
):
    sections, places, replicas = mesh_sizes
    chips = places // 2
    tokens, width = saved_inputs.shape[2:]
    hidden = up_weights.shape[1]
    cap = min(tokens, 3 * tokens // chips)
    half = width // 2
    block = 2 * cap
    per_step = chips * block
    group_slots = per_step // 8
    quarter = width // replicas
    vmem = pl.BlockSpec(memory_space=pltpu.VMEM)
    anywhere = pl.BlockSpec(memory_space=pl.ANY)
    dma = pltpu.SemaphoreType.DMA
    scratch = [
        pltpu.VMEM((hidden, width), bf16),
        pltpu.VMEM((hidden, width), bf16),
        pltpu.VMEM((tokens, width), bf16),
        pltpu.VMEM((tokens, width), bf16),
        pltpu.VMEM((2, tokens, width), bf16),
        pltpu.VMEM((1, width), bf16),
        pltpu.VMEM((2, 1, 2, tokens), jnp.int32),
        pltpu.VMEM((2, 1, 2, tokens), f32),
        pltpu.VMEM((5, chips * block, 2 * tokens), bf16),
        pltpu.VMEM((5, chips * block, 1), f32),
        pltpu.VMEM((2, 2, 2 * tokens, half), bf16),
        pltpu.VMEM((2, 2 * tokens, 1), f32),
        pltpu.VMEM((4, chips, block, half), bf16),
        pltpu.VMEM((4, chips, block, half), bf16),
        pltpu.VMEM((4, chips, block, half), bf16),
        pltpu.VMEM((3, chips, block, quarter // 2), bf16),
        pltpu.VMEM((3, chips, block, quarter // 2), bf16),
        pltpu.VMEM((3, chips, block, quarter // 2), bf16),
        pltpu.VMEM((2 * per_step, width), bf16),
        pltpu.VMEM((2 * per_step, width), bf16),
        pltpu.VMEM((2 * per_step, hidden), bf16),
        pltpu.VMEM((2 * per_step, hidden), bf16),
        pltpu.VMEM((per_step, hidden), f32),
        pltpu.VMEM((4, 2 * tokens), f32),
        pltpu.VMEM((3, 4, 2 * tokens), f32),
        pltpu.VMEM((3, 2 * tokens, quarter // 2), bf16),
        pltpu.VMEM((3, 2 * tokens, quarter // 2), bf16),
        pltpu.VMEM((3, per_step, hidden), bf16),
        pltpu.VMEM((3 * per_step, quarter), bf16),
        pltpu.VMEM((4, group_slots, width), f32),
        pltpu.VMEM((2, 4, group_slots, width), bf16),
        pltpu.VMEM((2, 4, group_slots, width), bf16),
        pltpu.VMEM((2, chips, block, half), bf16),
        pltpu.VMEM((2, chips, block, half), bf16),
        pltpu.VMEM((2 * tokens, half), bf16),
        pltpu.VMEM((2 * tokens, half), bf16),
        pltpu.VMEM((2, 2, hidden // 2, quarter), bf16),
        pltpu.VMEM((2, 2, hidden // 2, quarter), bf16),
        pltpu.VMEM((2, 2, 2, hidden // 2, quarter), bf16),
        pltpu.VMEM((2, 2, 2, hidden // 2, quarter), bf16),
        pltpu.VMEM((2, 2, hidden // 2, quarter), f32),
        dma((9,)),
        dma((7, chips)),
        dma((7, chips)),
        dma((7, chips)),
        dma((7, chips)),
        dma((2, 4)),
        dma((2, 4)),
        dma((2, chips)),
        dma((2, chips)),
        dma,
        dma,
        dma((2, 2)),
        dma((2, 2)),
        dma((2, 2, 2)),
        dma((2, 2, 2)),
        dma((3,)),
        dma((3,)),
        dma((3,)),
        dma((3,)),
        dma((4,)),
        dma((4,)),
    ]
    return tuple(
        pl.pallas_call(
            functools.partial(kernel, chips, replicas, sections, cap),
            out_shape=[
                pltpu.VMEM((2, 1, tokens, width), bf16),
                pltpu.VMEM((1, hidden, quarter), bf16),
                pltpu.VMEM((1, hidden, quarter), bf16),
            ],
            in_specs=[anywhere] * 8,
            out_specs=[vmem] * 3,
            scratch_shapes=scratch,
            compiler_params=pltpu.CompilerParams(
                collective_id=0, has_side_effects=True, vmem_limit_bytes=56 * 2**20
            ),
        )(
            in_flight,
            fresh_grads,
            saved_inputs,
            norm_gain,
            jnp.swapaxes(expert_ids, 2, 3),
            jnp.swapaxes(gate_weights, 2, 3),
            up_weights,
            down_weights,
        )
    )


def solution(mesh):
    in_specs = (
        P("pipe", ("expert", "dp"), None),
        P(None, ("expert", "dp"), None),
        P(None, "pipe", ("expert", "dp"), None),
        P("pipe", None),
        P(None, "pipe", ("expert", "dp"), None),
        P(None, "pipe", ("expert", "dp"), None),
        P("pipe", "expert", None),
        P("pipe", "expert", None),
    )
    out_specs = (
        P(None, "pipe", ("expert", "dp"), None),
        P("pipe", "expert", "dp"),
        P("pipe", "expert", "dp"),
    )
    sizes = tuple(mesh.shape[name] for name in ("pipe", "expert", "dp"))
    return jax.shard_map(
        functools.partial(local, sizes),
        mesh=mesh,
        in_specs=in_specs,
        out_specs=out_specs,
        check_vma=False,
    )
```
